32 devices in a mesh: groups: 2 (over x), req: 4 (over y, core), head: 4 (over z).
Axes of the slice: x: 2, y: 2, z: 4, core: 2. Of those that a mesh axis runs over, the one named last changes fastest.
Arguments:
- stretch_query: bfloat16 [2048, 12288], P(('groups', 'req'), 'head'), parts along dimension 0, may hold values from -48 to 48
- stretch_latent: bfloat16 [2048, 576], P(('groups', 'req')), parts along dimension 0, may hold values from -6 to 6
- cache_pool: bfloat16 [512, 36864], P(('groups', 'req'), 'head'), parts along dimension 0, may hold values from -6 to 6
- hit_slot: int32 [8, 16], P('groups'), parts along dimension 0, may hold values from 0 to 63
- hit_owner: int32 [8, 16], P('groups'), parts along dimension 0, may hold values from 0 to 3, as said below
- prefix_len: int32 [8], P('groups'), parts along dimension 0, may hold values from 768 to 1024, as said below
- head_mask: int32 [64], P('head'), may hold values 0 or 1
- up_key: bfloat16 [512, 8192], P(None, 'head'), may hold values from -0.25 to 0.25
- up_value: bfloat16 [512, 8192], P(None, 'head'), may hold values from -0.25 to 0.25
- out_weight: bfloat16 [5120, 8192], P('req', 'head'), may hold values from -0.5 to 0.5
Outputs:
- projected: bfloat16 [2048, 5120], P(('groups', 'req'), 'head'), parts along dimension 0
The draws below stay inside these ranges and needn't reach their ends.
There are 2 independent parts, one for each index of `groups`. The reference program is written for one: setup_inputs(seed, part) draws one part's arguments, and reference() takes and returns one part's arrays. A program takes and returns all parts, laid end to end along the dimension named above; an argument that names none is the same for every part. Nothing has to cross between parts.
Inputs may be any that keep to these rules, and one draw needn't show every extreme that they name: `hit_owner`: within one request's list no owner appears more than 6 times; in every request's list some owner appears exactly 6 times. `prefix_len`: multiples of 64; in every draw one request has 1024 and another the least.
All inputs are finite; a program needn't handle non-finite values. No bound on the sum of `head_mask` on one device may be relied on, other than what follows from the above.
Results may differ from the reference program's by a relative error of at most 0.0072.
Values may be sent and summed in bfloat16 or wider, within the bound.
No kernel may reach another device: no remote copies, remote signals or barrier semaphores. Data moves between devices by JAX's collectives and lax.ppermute only.
A program may use at most 128 MiB of HBM per device.

```python
import math
import jax
import jax.numpy as jnp
from jax import lax

D = 5120
HEADS = 64
KVR = 512
NOPE = 128
VD = 128
BT = 64
STRETCH = 256
KEYBLK = 4
BLK = 16
POOL_DEV = 64
LAT = 576
QKD = 192
REQS = 4
TOKENS = 1024
POOL = 256
N_REQ = 4


def draw_stretch_query(key, part):
    key = jax.random.fold_in(key, 1)
    values = 2.0 * jax.random.truncated_normal(key, -4.0, 4.0, (REQS, STRETCH, HEADS, QKD), jnp.float32)
    return values.reshape(TOKENS, HEADS * QKD).astype(jnp.bfloat16)


def draw_stretch_latent(key, part):
    key = jax.random.fold_in(key, 2)
    values = jax.random.truncated_normal(key, -6.0, 6.0, (REQS, STRETCH, LAT), jnp.float32)
    return values.reshape(TOKENS, LAT).astype(jnp.bfloat16)


def draw_hit_owner(key, part):
    key = jax.random.fold_in(key, 4)
    capacity = max(2, (BLK + N_REQ - 1) // N_REQ * 3 // 2)
    slot_count = N_REQ * capacity
    owner_of = jnp.arange(slot_count) // capacity

    def one_list(list_key):
        first_key, second_key, third_key = jax.random.split(list_key, 3)
        chosen = jax.random.randint(first_key, (), 0, N_REQ)
        ranking = jax.random.permutation(second_key, slot_count) - slot_count * (owner_of == chosen).astype(jnp.int32)
        ordering = jnp.argsort(ranking, stable=True)
        picked = owner_of[ordering[:BLK]]
        return picked[jax.random.permutation(third_key, BLK)]
    return jax.vmap(one_list)(jax.random.split(key, REQS)).astype(jnp.int32)


def draw_prefix_len(key, part):
    key = jax.random.fold_in(key, 5)
    first_key, second_key = jax.random.split(key)
    least = 3 * BLK // 4
    blocks = jax.random.randint(first_key, (REQS,), least, BLK + 1)
    longest = jax.random.randint(second_key, (), 0, REQS)
    shortest = (longest + 1) % REQS
    position = jnp.arange(REQS)
    blocks = jnp.where(position == longest, BLK, blocks)
    blocks = jnp.where(position == shortest, least, blocks)
    return (blocks * BT).astype(jnp.int32)


def set_ends(array, own_key, low, largest):
    longest = array.shape.index(max(array.shape))
    spots = []
    for shift in (0, 1):
        where = [jax.random.randint(jax.random.fold_in(own_key, axis), (), 0, length) for axis, length in enumerate(array.shape)]
        where[longest] = (where[longest] + shift) % array.shape[longest]
        spots.append(tuple(where))
    return array.at[spots[0]].set(low).at[spots[1]].set(largest)


def block_scale(own_key, dims, pieces, smallest, high):
    def one(dim, blocks):
        steps = jax.random.uniform(jax.random.fold_in(jax.random.fold_in(own_key, 6), dim), (blocks,), jnp.float32, smallest / len(pieces), high / len(pieces))
        return jnp.repeat(jnp.exp(steps), dims[dim] // blocks).reshape((-1,) + (1,) * (len(dims) - dim - 1))

    gain = one(*pieces[0])
    for cut in pieces[1:]:
        gain = gain * one(*cut)
    return gain


def scatter_about(rng, extent, width, reach, cuts=(), held_as=jnp.bfloat16):
    drawn = width * jax.random.normal(rng, extent, jnp.float32)
    if cuts:
        drawn = drawn * block_scale(rng, extent, cuts, -0.22, 0.18)
    return jnp.clip(drawn, -reach, reach).astype(held_as)


def setup_inputs(seed: int = 0, part: int = 0) -> dict:
    splits = jax.random.split(jax.random.key(seed), 11)
    own_keys = jax.random.split(jax.random.fold_in(splits[10], part), 11)
    return {
        "stretch_query": draw_stretch_query(jax.random.fold_in(jax.random.fold_in(splits[10], part), 71), part),
        "stretch_latent": draw_stretch_latent(jax.random.fold_in(jax.random.fold_in(splits[10], part), 71), part),
        "cache_pool": scatter_about(own_keys[2], (POOL, BT * LAT), 1.0, 6.0, ((0, 4), (1, 4))),
        "hit_slot": set_ends(jax.random.randint(own_keys[3], (REQS, BLK), 0, POOL_DEV), jax.random.fold_in(own_keys[3], 1), 0, POOL_DEV - 1).astype(jnp.int32),
        "hit_owner": draw_hit_owner(jax.random.fold_in(jax.random.fold_in(splits[10], part), 71), part),
        "prefix_len": draw_prefix_len(jax.random.fold_in(jax.random.fold_in(splits[10], part), 71), part),
        "head_mask": set_ends((jax.random.randint(splits[6], (HEADS,), 0, 4) < 3).astype(jnp.int32), jax.random.fold_in(splits[6], 1), 0, 1),
        "up_key": scatter_about(splits[7], (KVR, HEADS * NOPE), KVR ** -0.5, 0.25, ((1, 4),)),
        "up_value": scatter_about(splits[8], (KVR, HEADS * VD), KVR ** -0.5, 0.25, ((1, 4),)),
        "out_weight": scatter_about(splits[9], (D, HEADS * VD), VD ** -0.5, 0.5, ((0, 4), (1, 4))),
    }


def attend_block(carry_state, latent_block, allowed, query_nope, query_rope, up_key, up_value):
    running_max, row_total, weighted = carry_state
    local_heads = query_nope.shape[1]
    score_scale = 1.0 / math.sqrt(QKD)
    compressed = latent_block[:, :KVR]
    key_rope = latent_block[:, KVR:]
    key_nope = jnp.dot(compressed, up_key, preferred_element_type=jnp.float32).astype(jnp.bfloat16)
    key_nope = key_nope.reshape(-1, local_heads, NOPE)
    values = jnp.dot(compressed, up_value, preferred_element_type=jnp.float32).astype(jnp.bfloat16)
    values = values.reshape(-1, local_heads, VD)
    scores = jnp.einsum('qhn,khn->hqk', query_nope.astype(jnp.float32), key_nope.astype(jnp.float32))
    scores = scores + jnp.einsum('qhr,kr->hqk', query_rope.astype(jnp.float32), key_rope.astype(jnp.float32))
    scores = jnp.where(allowed[None], scores * score_scale, -1e+30)
    new_max = jnp.maximum(running_max, lax.optimization_barrier(jnp.max(scores, axis=2)))
    factor = jnp.exp(running_max - new_max)
    weights = jnp.exp(scores - new_max[:, :, None])
    row_total = row_total * factor + lax.optimization_barrier(jnp.sum(weights, axis=2))
    rounded = weights.astype(jnp.bfloat16)
    update = jnp.einsum('hqk,khv->qhv', rounded.astype(jnp.float32), values.astype(jnp.float32))
    weighted = weighted * jnp.transpose(factor)[:, :, None] + update
    return (new_max, row_total, weighted)

def reference(stretch_query, stretch_latent, cache_pool, hit_slot, hit_owner, prefix_len, head_mask, up_key, up_value, out_weight):
    queries = stretch_query.reshape(REQS, STRETCH, HEADS, QKD)
    latents = stretch_latent.reshape(REQS, STRETCH, LAT)
    span = KEYBLK * BT

    def one_request(inputs):
        query_rows, latent_rows, slots, owners, length = inputs
        rows_index = (owners * POOL_DEV + slots).astype(jnp.int32)
        prefix = jnp.take(cache_pool, rows_index, axis=0).reshape(BLK * BT, LAT)
        query_nope = query_rows[:, :, :NOPE]
        query_rope = query_rows[:, :, NOPE:]
        initial = (jnp.full((HEADS, STRETCH), -1e+30, jnp.float32), jnp.zeros((HEADS, STRETCH), jnp.float32), jnp.zeros((STRETCH, HEADS, VD), jnp.float32))
        block_steps = ((length + span - 1) // span).astype(jnp.int32)

        def prefix_step(step_index, carry_state):
            start_row = (step_index * span).astype(jnp.int32)
            latent_block = lax.dynamic_slice_in_dim(prefix, start_row, span, 0)
            key_index = start_row + jnp.arange(span).astype(jnp.int32)
            allowed = jnp.broadcast_to((key_index < length)[None, :], (STRETCH, span))
            return attend_block(carry_state, latent_block, allowed, query_nope, query_rope, up_key, up_value)
        carry_state = lax.fori_loop(jnp.int32(0), block_steps, prefix_step, initial)
        causal = jnp.arange(STRETCH)[None, :] <= jnp.arange(STRETCH)[:, None]
        running_max, row_total, weighted = attend_block(carry_state, latent_rows, causal, query_nope, query_rope, up_key, up_value)
        attended = (weighted / jnp.transpose(row_total)[:, :, None]).astype(jnp.bfloat16)
        attended = attended * head_mask.astype(jnp.bfloat16)[None, :, None]
        return attended.reshape(STRETCH, HEADS * VD)
    attended_all = lax.map(one_request, (queries, latents, hit_slot, hit_owner, prefix_len))
    attended_all = attended_all.reshape(TOKENS, HEADS * VD)
    return jnp.dot(attended_all, out_weight.T, preferred_element_type=jnp.float32).astype(jnp.bfloat16)
```

```python
import math

import jax
import jax.numpy as jnp
from jax import lax
from jax.experimental import pallas as pl
from jax.experimental.pallas import tpu as pltpu
from jax.sharding import PartitionSpec as P

KVR = 512
NOPE = 128
VD = 128
BT = 64
STRETCH = 256
BLK = 16
LAT = 576
QKD = 192
ROPE = LAT - KVR
MASKED = -1e30
BF16 = jnp.bfloat16
F32 = jnp.float32


def attention_kernel(
    blocks_ref, mask_ref, query_ref, stretch_ref, *refs, piece_count
):
    pieces = refs[:piece_count]
    key_ref, value_ref, out_ref, latent, rope = refs[piece_count:]
    step = pl.program_id(0)
    piece_tokens = pieces[0].shape[1] // LAT
    prefix = piece_count * piece_tokens * BLK
    total = prefix + STRETCH

    @pl.when(step == 0)
    def _():
        lane = lax.broadcasted_iota(jnp.int32, (BLK, ROPE), 1)
        row = lax.broadcasted_iota(jnp.int32, (BLK, ROPE), 0)
        hidden = (lane == 0) & (row >= blocks_ref[0])
        extra = jnp.where(hidden, MASKED, 0.0).astype(BF16)
        for index, piece in enumerate(pieces):
            for token in range(piece_tokens):
                start = (index * piece_tokens + token) * BLK
                base = LAT * token
                latent[start : start + BLK, :] = piece[:, base : base + KVR]
                rope[start : start + BLK, :] = jnp.concatenate(
                    [piece[:, base + KVR : base + LAT], extra], axis=1
                )
        latent[prefix:total, :] = stretch_ref[:, :KVR]
        rope[prefix:total, :] = jnp.concatenate(
            [stretch_ref[:, KVR:], jnp.zeros((STRETCH, ROPE), BF16)], axis=1
        )

    compressed = latent[...]
    keys = jnp.dot(compressed, key_ref[...], preferred_element_type=F32).astype(BF16)
    values = jnp.dot(compressed, value_ref[...], preferred_element_type=F32).astype(BF16)
    key_rope = rope[...]
    ones = jnp.ones((total, VD), BF16)
    lane = lax.broadcasted_iota(jnp.int32, (STRETCH, ROPE), 1)
    query_extra = jnp.where(lane == 0, 1.0, 0.0).astype(BF16)
    scale = 1.0 / (math.sqrt(QKD) * math.log(2.0))
    causal = lax.broadcasted_iota(jnp.int32, (STRETCH, STRETCH), 1) <= lax.broadcasted_iota(
        jnp.int32, (STRETCH, STRETCH), 0
    )
    for part in range(2):
        query = jnp.concatenate(
            [query_ref[:, part * QKD : (part + 1) * QKD], query_extra], axis=1
        )
        key = jnp.concatenate([keys[:, part * NOPE : (part + 1) * NOPE], key_rope], axis=1)
        scores = lax.dot_general(
            query, key, (((1,), (1,)), ((), ())), preferred_element_type=F32
        )
        before = scores[:, :prefix]
        own = jnp.where(causal, scores[:, prefix:], MASKED)
        largest = jnp.maximum(
            jnp.max(before, axis=1, keepdims=True), jnp.max(own, axis=1, keepdims=True)
        )
        weights = jnp.concatenate(
            [
                jnp.exp2((before - largest) * scale).astype(BF16),
                jnp.exp2((own - largest) * scale).astype(BF16),
            ],
            axis=1,
        )
        value = jnp.concatenate([values[:, part * VD : (part + 1) * VD], ones], axis=1)
        summed = jnp.dot(weights, value, preferred_element_type=F32)
        attended = (summed[:, :VD] / summed[:, VD:]).astype(BF16)
        kept = mask_ref[2 * step + part].astype(F32).astype(BF16)
        out_ref[:, part * VD : (part + 1) * VD] = attended * kept


def attention(blocks, head_mask, stretch_query, stretch_latent, pieces, up_key, up_value):
    heads = up_key.shape[1] // NOPE
    piece_tokens = pieces[0].shape[1] // LAT
    total = len(pieces) * piece_tokens * BLK + STRETCH

    def whole(array):
        return pl.BlockSpec(array.shape, lambda step: (0, 0))

    def columns(rows, width):
        return pl.BlockSpec((rows, width), lambda step: (0, step))

    smem = pl.BlockSpec(memory_space=pltpu.SMEM)
    return pl.pallas_call(
        lambda *refs: attention_kernel(*refs, piece_count=len(pieces)),
        grid=(heads // 2,),
        in_specs=[smem, smem, columns(STRETCH, 2 * QKD), whole(stretch_latent)]
        + [whole(piece) for piece in pieces]
        + [columns(KVR, 2 * NOPE), columns(KVR, 2 * VD)],
        out_specs=columns(STRETCH, 2 * VD),
        out_shape=jax.ShapeDtypeStruct((STRETCH, heads * VD), BF16),
        scratch_shapes=[
            pltpu.VMEM((total, KVR), BF16),
            pltpu.VMEM((total, 2 * ROPE), BF16),
        ],
        compiler_params=pltpu.CompilerParams(vmem_limit_bytes=48 * 1024 * 1024),
        cost_estimate=pl.CostEstimate(
            flops=2 * heads * total * VD * (2 * KVR + 4 * STRETCH),
            bytes_accessed=8 * 1024 * 1024,
            transcendentals=heads * total * STRETCH,
        ),
        name="attention",
    )(blocks, head_mask, stretch_query, stretch_latent, *pieces, up_key, up_value)


def hit_tables(hit_slot, hit_owner, prefix_len, own_req, capacity, sources, targets):
    block_index = jnp.arange(BLK)
    in_prefix = block_index[None, :] < (prefix_len // BT)[:, None]
    own_hits = in_prefix & (hit_owner == own_req)
    rank = jnp.cumsum(own_hits.astype(jnp.int32), axis=1) - 1
    chosen = own_hits[:, None, :] & (rank[:, None, :] == jnp.arange(capacity)[None, :, None])
    slots = jnp.sum(jnp.where(chosen, hit_slot[:, None, :], 0), axis=2)
    slots = jnp.take(slots, targets, axis=0)
    length = lax.dynamic_index_in_dim(prefix_len, own_req, 0, False)
    owners = lax.dynamic_index_in_dim(hit_owner, own_req, 0, False)
    from_source = (owners[:, None] == sources[None, :]) & (block_index < length // BT)[:, None]
    ranks = jnp.cumsum(from_source.astype(jnp.int32), axis=0) - 1
    picks = from_source[:, :, None] & (ranks[:, :, None] == jnp.arange(capacity)[None, None, :])
    return slots, picks.reshape(BLK, -1).astype(BF16), (length // BT).reshape(1)


def project_kernel(route_ref, attended_ref, *refs):
    weights, (mine_ref, other_ref, send_ref) = refs[:-3], refs[-3:]
    attended = attended_ref[...]
    own_half = route_ref[1]
    for unit in range(4):
        slot = unit ^ route_ref[0]
        if unit < 2:
            total = lax.dot_general(
                attended, weights[unit][...], (((1,), (1,)), ((), ())), preferred_element_type=F32
            )
        else:
            near, far = weights[2 * unit - 2], weights[2 * unit - 1]
            first, second = (
                lax.dot_general(
                    attended, piece[...], (((1,), (1,)), ((), ())), preferred_element_type=F32
                )
                for piece in (near, far)
            )
            swapped = own_half == 1
            total = jnp.concatenate(
                [jnp.where(swapped, second, first), jnp.where(swapped, first, second)], axis=1
            )

        @pl.when(slot == 0)
        def _():
            mine_ref[...] = total

        @pl.when(slot == 2)
        def _():
            other_ref[...] = total

        @pl.when(slot == 1)
        def _():
            send_ref[0] = total.astype(BF16)

        @pl.when(slot == 3)
        def _():
            send_ref[1] = total.astype(BF16)


def project(route, attended, own, beside, pieces, chunk, rows):
    width = attended.shape[1]
    half = rows // 2
    part = pl.BlockSpec((rows, width), lambda step: (chunk, 0))
    piece = pl.BlockSpec((half, width), lambda step: (0, 0))
    tokens = attended.shape[0]
    return pl.pallas_call(
        project_kernel,
        grid=(1,),
        in_specs=[
            pl.BlockSpec(memory_space=pltpu.SMEM),
            pl.BlockSpec(attended.shape, lambda step: (0, 0)),
            part,
            part,
            piece,
            piece,
            piece,
            piece,
        ],
        out_specs=[
            pl.BlockSpec((tokens, rows), lambda step: (0, 0)),
            pl.BlockSpec((tokens, rows), lambda step: (0, 0)),
            pl.BlockSpec((2, tokens, rows), lambda step: (0, 0, 0)),
        ],
        out_shape=[
            jax.ShapeDtypeStruct((tokens, rows), F32),
            jax.ShapeDtypeStruct((tokens, rows), F32),
            jax.ShapeDtypeStruct((2, tokens, rows), BF16),
        ],
        compiler_params=pltpu.CompilerParams(vmem_limit_bytes=48 * 1024 * 1024),
        cost_estimate=pl.CostEstimate(
            flops=8 * tokens * rows * width, bytes_accessed=8 * rows * width, transcendentals=0
        ),
        name="project",
    )(route, attended, own, beside, *pieces)


def flip(size, bit):
    return [(index, index ^ bit) for index in range(size)]


def local(
    stretch_query,
    stretch_latent,
    cache_pool,
    hit_slot,
    hit_owner,
    prefix_len,
    head_mask,
    up_key,
    up_value,
    out_weight,
):
    groups = lax.axis_size("groups")
    req_count = lax.axis_size("req")
    head_count = lax.axis_size("head")
    capacity = max(2, (BLK + req_count - 1) // req_count * 3 // 2)
    own_req = lax.axis_index("req")
    own_head = lax.axis_index("head")
    paired = groups == 2 and req_count == 4 and head_count == 4
    order = jnp.arange(req_count)
    partners = order ^ own_req if paired else order
    slots, picks, blocks = hit_tables(
        hit_slot, hit_owner, prefix_len, own_req, capacity, partners, partners
    )
    if not paired:
        outgoing = jnp.take(cache_pool, slots.reshape(-1), axis=0)
        incoming = lax.all_to_all(outgoing, "req", split_axis=0, concat_axis=0, tiled=True)
        prefix = jnp.dot(picks, incoming, preferred_element_type=F32).astype(BF16)
        gathered = lax.all_gather(prefix, "head", axis=0)
        pieces = [gathered[index] for index in range(head_count)]
        attended = attention(
            blocks, head_mask, stretch_query, stretch_latent, pieces, up_key, up_value
        )
        partial_out = lax.dot_general(
            attended,
            lax.all_gather(out_weight, "req", axis=0, tiled=True),
            (((1,), (1,)), ((), ())),
            preferred_element_type=F32,
        )
        return lax.psum_scatter(partial_out, "head", scatter_dimension=1, tiled=True).astype(BF16)

    own_group = lax.axis_index("groups")
    outgoing = [jnp.take(cache_pool, slots[index], axis=0) for index in range(req_count)]
    incoming = [outgoing[0]] + [
        lax.ppermute(outgoing[bit], "req", flip(req_count, bit)) for bit in (1, 2, 3)
    ]
    prefix = jnp.dot(
        picks, jnp.concatenate(incoming, axis=0), preferred_element_type=F32
    ).astype(BF16)
    far = lax.ppermute(prefix, "head", flip(head_count, 2))
    near = lax.ppermute(prefix, "head", flip(head_count, 1))
    farther = lax.ppermute(far, "head", flip(head_count, 1))

    rows = 256
    chunks = out_weight.shape[0] // rows
    half = rows // 2
    beside = lax.ppermute(out_weight, "req", flip(req_count, 1))
    across = []
    for chunk in range(chunks):
        piece = lax.dynamic_slice_in_dim(
            out_weight, chunk * rows + own_group * half, half, 0
        )
        first = lax.ppermute(piece, "req", flip(req_count, 2))
        second = lax.ppermute(first, "groups", flip(groups, 1))
        across.append(
            (
                first,
                second,
                lax.ppermute(first, "req", flip(req_count, 1)),
                lax.ppermute(second, "req", flip(req_count, 1)),
            )
        )

    attended = attention(
        blocks,
        head_mask,
        stretch_query,
        stretch_latent,
        [prefix, near, far, farther],
        up_key,
        up_value,
    )
    route = jnp.stack([own_req ^ own_head, own_group]).astype(jnp.int32)
    outs = []
    for chunk in range(chunks):
        mine, other, send = project(
            route, attended, out_weight, beside, across[chunk], chunk, rows
        )
        received = lax.ppermute(send, "head", flip(head_count, 1))
        passed = lax.ppermute(
            (other + received[1].astype(F32)).astype(BF16), "head", flip(head_count, 2)
        )
        outs.append((mine + received[0].astype(F32) + passed.astype(F32)).astype(BF16))
    return jnp.concatenate(outs, axis=1)


def solution(mesh):
    placed = (
        P(("groups", "req"), "head"),
        P(("groups", "req"), None),
        P(("groups", "req"), "head"),
        P("groups", None),
        P("groups", None),
        P("groups"),
        P("head"),
        P(None, "head"),
        P(None, "head"),
        P("req", "head"),
    )
    return jax.shard_map(
        local, mesh=mesh, in_specs=placed, out_specs=P(("groups", "req"), "head"), check_vma=False
    )
```

```python
import math

import jax
import jax.numpy as jnp
from jax import lax
from jax.experimental import pallas as pl
from jax.experimental.pallas import tpu as pltpu
from jax.sharding import PartitionSpec as P

KVR = 512
NOPE = 128
VD = 128
BT = 64
STRETCH = 256
BLK = 16
LAT = 576
QKD = 192
ROPE = LAT - KVR
MASKED = -1e30
PIECES = (192, 288, 256, 256, 288)
STEPS = (2, 2, 1)
VMEM_BYTES = 60 * 1024 * 1024
SMALL_COST = pl.CostEstimate(flops=1024, bytes_accessed=1024, transcendentals=0)
BF16 = jnp.bfloat16
F32 = jnp.float32


def attention_kernel(blocks_ref, mask_ref, query_ref, stretch_ref, *refs, together, skipped):
    *pieces, key_ref, value_ref, out_ref, latent, rope = refs
    step = pl.program_id(0)
    piece_tokens = pieces[0].shape[1] // LAT
    prefix = len(pieces) * piece_tokens * BLK
    total = prefix + STRETCH

    @pl.when(step == 0)
    def _():
        lane = lax.broadcasted_iota(jnp.int32, (BLK, ROPE), 1)
        row = lax.broadcasted_iota(jnp.int32, (BLK, ROPE), 0)
        hidden = (lane == 0) & (row >= blocks_ref[0])
        extra = jnp.where(hidden, MASKED, 0.0).astype(BF16)
        for index, piece in enumerate(pieces):
            for token in range(piece_tokens):
                start = (index * piece_tokens + token) * BLK
                base = LAT * token
                latent[start : start + BLK, :] = piece[:, base : base + KVR]
                rope[start : start + BLK, :] = jnp.concatenate(
                    [piece[:, base + KVR : base + LAT], extra], axis=1
                )
        latent[prefix:total, :] = stretch_ref[:, :KVR]
        rope[prefix:total, :] = jnp.concatenate(
            [stretch_ref[:, KVR:], jnp.zeros((STRETCH, ROPE), BF16)], axis=1
        )

    compressed = latent[...]
    keys = jnp.dot(compressed, key_ref[...], preferred_element_type=F32).astype(BF16)
    values = jnp.dot(compressed, value_ref[...], preferred_element_type=F32).astype(BF16)
    key_rope = rope[...]
    ones = jnp.ones((total, VD), BF16)
    lane = lax.broadcasted_iota(jnp.int32, (STRETCH, ROPE), 1)
    query_extra = jnp.where(lane == 0, 1.0, 0.0).astype(BF16)
    scale = 1.0 / (math.sqrt(QKD) * math.log(2.0))
    causal = lax.broadcasted_iota(jnp.int32, (STRETCH, STRETCH), 1) <= lax.broadcasted_iota(
        jnp.int32, (STRETCH, STRETCH), 0
    )
    for part in range(together):
        here = slice(part * VD, (part + 1) * VD)
        query = jnp.concatenate(
            [query_ref[:, part * QKD : (part + 1) * QKD], query_extra], axis=1
        )
        key = jnp.concatenate([keys[:, here], key_rope], axis=1)
        scores = lax.dot_general(
            query, key, (((1,), (1,)), ((), ())), preferred_element_type=F32
        )
        before = scores[:, :prefix]
        own = jnp.where(causal, scores[:, prefix:], MASKED)
        largest = jnp.maximum(
            jnp.max(before, axis=1, keepdims=True), jnp.max(own, axis=1, keepdims=True)
        )
        weights = jnp.concatenate(
            [
                jnp.exp2((before - largest) * scale).astype(BF16),
                jnp.exp2((own - largest) * scale).astype(BF16),
            ],
            axis=1,
        )
        value = jnp.concatenate([values[:, here], ones], axis=1)
        summed = jnp.dot(weights, value, preferred_element_type=F32)
        attended = (summed[:, :VD] / summed[:, VD:]).astype(BF16)
        kept = mask_ref[together * (step + skipped) + part].astype(F32).astype(BF16)
        out_ref[:, here] = attended * kept


def attention(blocks, head_mask, query, latent, pieces, up_key, up_value, part=0, parts=1):
    heads = up_key.shape[1] // NOPE // parts
    together = math.gcd(heads, 4)
    skipped = part * (heads // together)
    piece_tokens = pieces[0].shape[1] // LAT
    total = len(pieces) * piece_tokens * BLK + STRETCH

    def whole(array):
        return pl.BlockSpec(array.shape, lambda step: (0, 0))

    def columns(rows, width):
        return pl.BlockSpec((rows, together * width), lambda step: (0, step + skipped))

    smem = pl.BlockSpec(memory_space=pltpu.SMEM)
    return pl.pallas_call(
        lambda *refs: attention_kernel(*refs, together=together, skipped=skipped),
        grid=(heads // together,),
        in_specs=[smem, smem, columns(STRETCH, QKD)]
        + [whole(array) for array in [latent, *pieces]]
        + [columns(KVR, NOPE), columns(KVR, VD)],
        out_specs=pl.BlockSpec((STRETCH, together * VD), lambda step: (0, step)),
        out_shape=jax.ShapeDtypeStruct((STRETCH, heads * VD), BF16),
        scratch_shapes=[
            pltpu.VMEM((total, KVR), BF16),
            pltpu.VMEM((total, 2 * ROPE), BF16),
        ],
        compiler_params=pltpu.CompilerParams(vmem_limit_bytes=VMEM_BYTES),
        cost_estimate=pl.CostEstimate(
            flops=18_000_000_000 // parts, bytes_accessed=4 * 1024 * 1024, transcendentals=0
        ),
        name="attention",
    )(blocks, head_mask, query, latent, *pieces, up_key, up_value)


def hit_tables(hit_slot, hit_owner, prefix_len, own_req, capacity, sources, stride):
    block_index = jnp.arange(BLK)
    in_prefix = block_index[None, :] < (prefix_len // BT)[:, None]
    own_hits = in_prefix & (hit_owner == own_req)
    rank = jnp.cumsum(own_hits.astype(jnp.int32), axis=1) - 1
    chosen = own_hits[:, None, :] & (rank[:, None, :] == jnp.arange(capacity)[None, :, None])
    slots = jnp.sum(jnp.where(chosen, hit_slot[:, None, :], 0), axis=2)
    length = lax.dynamic_index_in_dim(prefix_len, own_req, 0, False)
    owners = lax.dynamic_index_in_dim(hit_owner, own_req, 0, False)
    from_source = (owners[:, None] == sources[None, :]) & (block_index < length // BT)[:, None]
    ranks = jnp.cumsum(from_source.astype(jnp.int32), axis=0) - 1
    picks = from_source[:, :, None] & (ranks[:, :, None] == jnp.arange(stride)[None, None, :])
    return slots, picks.reshape(BLK, -1).astype(BF16), (length // BT).reshape(1)


def refs_by_piece(refs, counts):
    refs = list(refs)
    return [[refs.pop(0) for _ in range(count)] for count in counts]


def project_kernel(route_ref, *refs, start, rows, pair_counts):
    halves, weight_hbm, refs = refs[:4], refs[4], refs[5:]
    pieces = refs[:-5]
    out_ref, attended, weights, totals, sems = refs[-5:]
    turn, group = route_ref[0], route_ref[1]
    tokens, width = halves[0].shape
    copies = [
        (halves[0], attended.at[:tokens, :width]),
        (halves[1], attended.at[:tokens, width:]),
        (weight_hbm.at[pl.ds(start, rows)], weights.at[0]),
        (halves[2], attended.at[tokens:, :width]),
        (halves[3], attended.at[tokens:, width:]),
    ]
    place = 0
    for pair in refs_by_piece(pieces, pair_counts):
        size = sum(piece.shape[0] for piece in pair)
        for index, piece in enumerate(pair):
            half = piece.shape[0]
            offset = place + ((group if index == 0 else 1 - group) * half if len(pair) == 2 else 0)
            copies.append((piece, weights.at[1, pl.ds(pl.multiple_of(offset, 16), half)]))
        place += size
    copies = [
        pltpu.make_async_copy(source, target, sems.at[index])
        for index, (source, target) in enumerate(copies)
    ]
    last = tuple(range(5, len(copies)))
    needs = ((0, 0, (0, 1, 2), (3, 4) + last), (0, 1, (3, 4), ()), (1, 0, last, ()), (1, 1, (), ()))
    for index in needs[0][2]:
        copies[index].start()
    for unit, request, awaited, following in needs:
        for index in awaited:
            copies[index].wait()
        for index in following:
            copies[index].start()
        span = slice(request * tokens, (request + 1) * tokens)
        totals[unit ^ turn, :, span] = lax.dot_general(
            weights[unit], attended[span], (((1,), (1,)), ((), ())), preferred_element_type=F32
        )
    for slot in range(2):
        out_ref[slot] = totals[slot].astype(BF16)


def project(route, halves, weight, pieces, start, rows):
    tokens, width = halves[0].shape[0], weight.shape[1]
    flat = [piece for pair in pieces for piece in pair]
    hbm = pl.BlockSpec(memory_space=pl.ANY)
    return pl.pallas_call(
        lambda *refs: project_kernel(
            *refs, start=start, rows=rows, pair_counts=[len(pair) for pair in pieces]
        ),
        in_specs=[pl.BlockSpec(memory_space=pltpu.SMEM)] + [hbm] * (5 + len(flat)),
        out_specs=pl.BlockSpec(memory_space=pltpu.VMEM),
        out_shape=jax.ShapeDtypeStruct((2, rows, 2 * tokens), BF16),
        scratch_shapes=[
            pltpu.VMEM((2 * tokens, width), BF16),
            pltpu.VMEM((2, rows, width), BF16),
            pltpu.VMEM((2, rows, 2 * tokens), F32),
            pltpu.SemaphoreType.DMA((5 + len(flat),)),
        ],
        compiler_params=pltpu.CompilerParams(vmem_limit_bytes=VMEM_BYTES),
        cost_estimate=pl.CostEstimate(
            flops=5_000_000_000, bytes_accessed=4 * 1024 * 1024, transcendentals=0
        ),
        name="project",
    )(route, *halves, weight, *flat)


def finish_kernel(route_ref, *refs, starts, sizes):
    out_ref = refs[-1]
    kept = route_ref[2] == 1
    for index, (start, rows) in enumerate(zip(starts, sizes)):
        own, other = refs[2 * index : 2 * index + 2]

        @pl.when(kept)
        def _():
            out_ref[:, start : start + rows] = own[...].astype(F32).T.astype(BF16)

        @pl.when(jnp.logical_not(kept))
        def _():
            out_ref[:, start : start + rows] = other[...].astype(F32).T.astype(BF16)


def finish(route, sums, starts, sizes):
    vmem = pl.BlockSpec(memory_space=pltpu.VMEM)
    tokens = sums[0].shape[1]
    return pl.pallas_call(
        lambda *refs: finish_kernel(*refs, starts=starts, sizes=sizes),
        in_specs=[pl.BlockSpec(memory_space=pltpu.SMEM)] + [vmem] * len(sums),
        out_specs=vmem,
        out_shape=jax.ShapeDtypeStruct((tokens, sum(sizes)), BF16),
        compiler_params=pltpu.CompilerParams(vmem_limit_bytes=VMEM_BYTES),
        cost_estimate=SMALL_COST,
        name="finish",
    )(route, *sums)


def pick_kernel(self_ref, owner_ref, slot_ref, length_ref, pool_ref, *refs, capacity):
    outs, table = refs[:-1], refs[-1]
    requests = len(outs)
    own = self_ref[0]
    rows = pool_ref.shape[0]
    lane = lax.broadcasted_iota(jnp.int32, (8, rows), 1)
    row = lax.broadcasted_iota(jnp.int32, (8, rows), 0)
    for bit in range(requests):
        target = own ^ bit
        blocks = length_ref[target] // BT
        for rank in range(capacity):
            table[rank] = 0

        def note(block, count):
            owned = (owner_ref[target, block] == own) & (block < blocks)

            @pl.when(owned & (count < capacity))
            def _():
                table[count] = slot_ref[target, block]

            return count + owned.astype(jnp.int32)

        lax.fori_loop(0, BLK, note, jnp.int32(0), unroll=True)
        chosen = jnp.zeros((8, rows), F32)
        for rank in range(capacity):
            chosen = jnp.where((row == rank) & (lane == table[rank]), 1.0, chosen)
        outs[bit][...] = jnp.dot(
            chosen.astype(BF16), pool_ref[...], preferred_element_type=F32
        ).astype(BF16)


def pick(own_req, hit_owner, hit_slot, prefix_len, cache_pool, capacity):
    requests = hit_owner.shape[0]
    smem = pl.BlockSpec(memory_space=pltpu.SMEM)
    vmem = pl.BlockSpec(memory_space=pltpu.VMEM)
    return pl.pallas_call(
        lambda *refs: pick_kernel(*refs, capacity=capacity),
        in_specs=[smem] * 4 + [vmem],
        out_specs=[vmem] * requests,
        out_shape=[jax.ShapeDtypeStruct((8, cache_pool.shape[1]), BF16)] * requests,
        scratch_shapes=[pltpu.SMEM((capacity,), jnp.int32)],
        compiler_params=pltpu.CompilerParams(vmem_limit_bytes=VMEM_BYTES),
        cost_estimate=SMALL_COST,
        name="pick",
    )(own_req.reshape(1), hit_owner, hit_slot, prefix_len, cache_pool)


def after(value, *earlier):
    return lax.optimization_barrier((value, *earlier))[0] if earlier else value


def flip(size, bit):
    return [(index, index ^ bit) for index in range(size)]


def local(
    stretch_query,
    stretch_latent,
    cache_pool,
    hit_slot,
    hit_owner,
    prefix_len,
    head_mask,
    up_key,
    up_value,
    out_weight,
):
    groups = lax.axis_size("groups")
    req_count = lax.axis_size("req")
    head_count = lax.axis_size("head")
    capacity = max(2, (BLK + req_count - 1) // req_count * 3 // 2)
    own_req = lax.axis_index("req")
    own_head = lax.axis_index("head")
    paired = groups == 2 and req_count == 4 and head_count == 4 and sum(PIECES) == out_weight.shape[0]
    order = jnp.arange(req_count)
    partners = order ^ own_req if paired else order
    slots, picks, blocks = hit_tables(
        hit_slot, hit_owner, prefix_len, own_req, capacity, partners, 8 if paired else capacity
    )
    if not paired:
        outgoing = jnp.take(cache_pool, slots.reshape(-1), axis=0)
        incoming = lax.all_to_all(outgoing, "req", split_axis=0, concat_axis=0, tiled=True)
        prefix = jnp.dot(picks, incoming, preferred_element_type=F32).astype(BF16)
        gathered = lax.all_gather(prefix, "head", axis=0)
        pieces = [gathered[index] for index in range(head_count)]
        attended = attention(
            blocks, head_mask, stretch_query, stretch_latent, pieces, up_key, up_value
        )
        partial_out = lax.dot_general(
            attended,
            lax.all_gather(out_weight, "req", axis=0, tiled=True),
            (((1,), (1,)), ((), ())),
            preferred_element_type=F32,
        )
        return lax.psum_scatter(partial_out, "head", scatter_dimension=1, tiled=True).astype(BF16)

    own_group = lax.axis_index("groups")
    sizes = PIECES
    starts = [sum(sizes[:index]) for index in range(len(sizes))]

    def over_y(chunk, *earlier):
        size = sizes[chunk]
        weights = after(out_weight, *earlier)
        if chunk == len(sizes) - 1:
            piece = lax.slice_in_dim(weights, starts[chunk], starts[chunk] + size, axis=0)
        else:
            half = size // 2
            piece = lax.dynamic_slice_in_dim(weights, starts[chunk] + own_group * half, half, 0)
        return lax.ppermute(piece, "req", flip(req_count, 2))

    def over_x(piece, *earlier):
        return lax.ppermute(after(piece, *earlier), "groups", flip(groups, 1))

    def over_z(piece, bit):
        return lax.ppermute(piece, "head", flip(head_count, bit))

    outgoing = pick(own_req, hit_owner, hit_slot, prefix_len, cache_pool, capacity)
    incoming = [outgoing[0]] + [
        lax.ppermute(outgoing[bit], "req", flip(req_count, bit)) for bit in (1, 2, 3)
    ]
    y0 = over_y(0, *outgoing)
    y1 = over_y(1, incoming[1])
    prefix = jnp.dot(
        picks, jnp.concatenate(incoming, axis=0), preferred_element_type=F32
    ).astype(BF16)
    far = over_z(prefix, 2)
    near = over_z(prefix, 1)
    farther = over_z(after(far, near, y1), 1)
    x0 = over_x(y0, far)
    x1 = over_x(y1)
    y2 = over_y(2, y1)

    def attend(part, *earlier):
        return attention(
            blocks,
            head_mask,
            after(stretch_query, *earlier),
            stretch_latent,
            [prefix, near, far, farther],
            up_key,
            up_value,
            part,
            2,
        )

    def over_core(piece):
        return lax.ppermute(piece, "req", flip(req_count, 1))

    first = attend(0, x0)
    second = attend(1, first, x1, y2)
    beside = over_core(first)
    x2 = over_x(y2)
    y3 = over_y(3, y2)
    halves = (first, second, beside, over_core(after(second, beside)))

    core = own_req & 1
    keeper = (own_head & 1) == core
    route = jnp.stack([(own_head >> 1) ^ (own_req >> 1), own_group, keeper]).astype(jnp.int32)
    devices = [(req, head) for req in range(req_count) for head in range(head_count)]

    def place(req, head):
        return req * head_count + head

    to_keeper = [
        (place(req, head), place(req, head ^ 1)) for req, head in devices if (req ^ head) & 1
    ]
    to_far = [
        (place(req, head), place(req, head ^ 2)) for req, head in devices if not (req ^ head) & 1
    ]
    to_core = [
        (place(req, head), place(req ^ 1, head)) for req, head in devices if not (req ^ head) & 1
    ]
    axes = ("req", "head")

    bounds = [sum(STEPS[:index]) for index in range(len(STEPS) + 1)]
    spans = [
        (starts[first], sum(sizes[first:last])) for first, last in zip(bounds[:-1], bounds[1:])
    ]

    def send(chunk, pieces, *earlier):
        sums = project(after(route, *earlier), halves, out_weight, pieces, *spans[chunk])
        return sums, lax.ppermute(sums, axes, to_keeper)

    def halve(sums, received):
        total = (sums[1].astype(F32) + received[1].astype(F32)).astype(BF16)
        return total, lax.ppermute(total, axes, to_far)

    def settle(sums, received, passed):
        total = sums[0].astype(F32) + received[0].astype(F32) + passed.astype(F32)
        return total.astype(BF16)

    def split(total):
        own, other = total[:, :STRETCH], total[:, STRETCH:]
        return [own, lax.ppermute(other, axes, to_core)]

    sums0, got0 = send(0, [(y0, x0), (y1, x1)], x2)
    x3 = over_x(y3)
    y4 = over_y(4, y3)
    total0, passed0 = halve(sums0, got0)
    sums1, got1 = send(1, [(y2, x2), (y3, x3)], sums0)
    sums2, got2 = send(2, [(y4,)], sums1, total0)
    total1, passed1 = halve(sums1, after(got1, passed0))
    total2, passed2 = halve(sums2, got2)
    early = [settle(sums0, got0, passed0), settle(sums1, got1, passed1)]
    settled = split(jnp.concatenate(early, axis=0)) + split(settle(sums2, got2, passed2))
    return finish(route, settled, (0, spans[2][0]), spans[2])


def solution(mesh):
    placed = (
        P(("groups", "req"), "head"),
        P(("groups", "req"), None),
        P(("groups", "req"), "head"),
        P("groups", None),
        P("groups", None),
        P("groups"),
        P("head"),
        P(None, "head"),
        P(None, "head"),
        P("req", "head"),
    )
    return jax.shard_map(
        local, mesh=mesh, in_specs=placed, out_specs=P(("groups", "req"), "head"), check_vma=False
    )
```

```python
import math

import jax
import jax.numpy as jnp
from jax import lax
from jax.experimental import pallas as pl
from jax.experimental.pallas import tpu as pltpu
from jax.sharding import PartitionSpec as P

KVR = 512
NOPE = 128
VD = 128
BT = 64
STRETCH = 256
BLK = 16
LAT = 576
QKD = 192
ROPE = LAT - KVR
MASKED = -1e30
PIECES = (448, 416, 224, 192)
STEPS = (1, 1, 1, 1)
WHOLE = 2
VMEM_BYTES = 60 * 1024 * 1024
LESS_VMEM_BYTES = 20 * 1024 * 1024
SMALL_COST = pl.CostEstimate(flops=1024, bytes_accessed=1024, transcendentals=0)
BF16 = jnp.bfloat16
F32 = jnp.float32


def attention_kernel(blocks_ref, mask_ref, query_ref, stretch_ref, *refs, together, skipped):
    *pieces, key_ref, value_ref, out_ref, latent, rope = refs
    step = pl.program_id(0)
    piece_tokens = pieces[0].shape[1] // LAT
    prefix = len(pieces) * piece_tokens * BLK
    total = prefix + STRETCH

    @pl.when(step == 0)
    def _():
        lane = lax.broadcasted_iota(jnp.int32, (BLK, ROPE), 1)
        row = lax.broadcasted_iota(jnp.int32, (BLK, ROPE), 0)
        hidden = (lane == 0) & (row >= blocks_ref[0])
        extra = jnp.where(hidden, MASKED, 0.0).astype(BF16)
        for index, piece in enumerate(pieces):
            for token in range(piece_tokens):
                start = (index * piece_tokens + token) * BLK
                base = LAT * token
                latent[start : start + BLK, :] = piece[:, base : base + KVR]
                rope[start : start + BLK, :] = jnp.concatenate(
                    [piece[:, base + KVR : base + LAT], extra], axis=1
                )
        latent[prefix:total, :] = stretch_ref[:, :KVR]
        rope[prefix:total, :] = jnp.concatenate(
            [stretch_ref[:, KVR:], jnp.zeros((STRETCH, ROPE), BF16)], axis=1
        )

    compressed = latent[...]
    keys = jnp.dot(compressed, key_ref[...], preferred_element_type=F32).astype(BF16)
    values = jnp.dot(compressed, value_ref[...], preferred_element_type=F32).astype(BF16)
    key_rope = rope[...]
    ones = jnp.ones((total, VD), BF16)
    lane = lax.broadcasted_iota(jnp.int32, (STRETCH, ROPE), 1)
    query_extra = jnp.where(lane == 0, 1.0, 0.0).astype(BF16)
    scale = 1.0 / (math.sqrt(QKD) * math.log(2.0))
    causal = lax.broadcasted_iota(jnp.int32, (STRETCH, STRETCH), 1) <= lax.broadcasted_iota(
        jnp.int32, (STRETCH, STRETCH), 0
    )
    for part in range(together):
        here = slice(part * VD, (part + 1) * VD)
        query = jnp.concatenate(
            [query_ref[:, part * QKD : (part + 1) * QKD], query_extra], axis=1
        )
        key = jnp.concatenate([keys[:, here], key_rope], axis=1)
        scores = lax.dot_general(
            query, key, (((1,), (1,)), ((), ())), preferred_element_type=F32
        )
        before = scores[:, :prefix]
        own = jnp.where(causal, scores[:, prefix:], MASKED)
        largest = jnp.maximum(
            jnp.max(before, axis=1, keepdims=True), jnp.max(own, axis=1, keepdims=True)
        )
        weights = jnp.concatenate(
            [
                jnp.exp2((before - largest) * scale).astype(BF16),
                jnp.exp2((own - largest) * scale).astype(BF16),
            ],
            axis=1,
        )
        value = jnp.concatenate([values[:, here], ones], axis=1)
        summed = jnp.dot(weights, value, preferred_element_type=F32)
        attended = (summed[:, :VD] / summed[:, VD:]).astype(BF16)
        kept = mask_ref[together * (step + skipped) + part].astype(F32).astype(BF16)
        out_ref[:, here] = attended * kept


def attention(blocks, head_mask, query, latent, pieces, up_key, up_value, part=0, parts=1):
    heads = up_key.shape[1] // NOPE // parts
    together = math.gcd(heads, 4)
    skipped = part * (heads // together)
    piece_tokens = pieces[0].shape[1] // LAT
    total = len(pieces) * piece_tokens * BLK + STRETCH

    def whole(array):
        return pl.BlockSpec(array.shape, lambda step: (0, 0))

    def columns(rows, width):
        return pl.BlockSpec((rows, together * width), lambda step: (0, step + skipped))

    smem = pl.BlockSpec(memory_space=pltpu.SMEM)
    return pl.pallas_call(
        lambda *refs: attention_kernel(*refs, together=together, skipped=skipped),
        grid=(heads // together,),
        in_specs=[smem, smem, columns(STRETCH, QKD)]
        + [whole(array) for array in [latent, *pieces]]
        + [columns(KVR, NOPE), columns(KVR, VD)],
        out_specs=pl.BlockSpec((STRETCH, together * VD), lambda step: (0, step)),
        out_shape=jax.ShapeDtypeStruct((STRETCH, heads * VD), BF16),
        scratch_shapes=[
            pltpu.VMEM((total, KVR), BF16),
            pltpu.VMEM((total, 2 * ROPE), BF16),
        ],
        compiler_params=pltpu.CompilerParams(vmem_limit_bytes=VMEM_BYTES),
        cost_estimate=pl.CostEstimate(
            flops=18_000_000_000 // parts, bytes_accessed=4 * 1024 * 1024, transcendentals=0
        ),
        name="attention",
    )(blocks, head_mask, query, latent, *pieces, up_key, up_value)


def hit_tables(hit_slot, hit_owner, prefix_len, own_req, capacity, sources, stride):
    block_index = jnp.arange(BLK)
    in_prefix = block_index[None, :] < (prefix_len // BT)[:, None]
    own_hits = in_prefix & (hit_owner == own_req)
    rank = jnp.cumsum(own_hits.astype(jnp.int32), axis=1) - 1
    chosen = own_hits[:, None, :] & (rank[:, None, :] == jnp.arange(capacity)[None, :, None])
    slots = jnp.sum(jnp.where(chosen, hit_slot[:, None, :], 0), axis=2)
    length = lax.dynamic_index_in_dim(prefix_len, own_req, 0, False)
    owners = lax.dynamic_index_in_dim(hit_owner, own_req, 0, False)
    from_source = (owners[:, None] == sources[None, :]) & (block_index < length // BT)[:, None]
    ranks = jnp.cumsum(from_source.astype(jnp.int32), axis=0) - 1
    picks = from_source[:, :, None] & (ranks[:, :, None] == jnp.arange(stride)[None, None, :])
    return slots, picks.reshape(BLK, -1).astype(BF16), (length // BT).reshape(1)


def refs_by_piece(refs, counts):
    refs = list(refs)
    return [[refs.pop(0) for _ in range(count)] for count in counts]


def project_kernel(route_ref, *refs, rows, pair_counts):
    own, beside, weight_hbm, refs = refs[0], refs[1], refs[2], refs[3:]
    pieces = refs[:-5]
    out_ref, attended, weights, totals, sems = refs[-5:]
    turn, group = route_ref[0], route_ref[1]
    tokens = own.shape[0]
    copies = [
        (own, attended.at[:tokens]),
        (weight_hbm, weights.at[0]),
        (beside, attended.at[tokens:]),
    ]
    place = 0
    for pair in refs_by_piece(pieces, pair_counts):
        size = sum(piece.shape[0] for piece in pair)
        for index, piece in enumerate(pair):
            half = piece.shape[0]
            offset = place + ((group if index == 0 else 1 - group) * half if len(pair) == 2 else 0)
            copies.append((piece, weights.at[1, pl.ds(pl.multiple_of(offset, 16), half)]))
        place += size
    copies = [
        pltpu.make_async_copy(source, target, sems.at[index])
        for index, (source, target) in enumerate(copies)
    ]
    last = tuple(range(3, len(copies)))
    needs = ((0, 0, (0, 1), (2,) + last), (0, 1, (2,), ()), (1, 0, last, ()), (1, 1, (), ()))
    for index in needs[0][2]:
        copies[index].start()
    for unit, request, awaited, following in needs:
        for index in awaited:
            copies[index].wait()
        for index in following:
            copies[index].start()
        span = slice(request * tokens, (request + 1) * tokens)
        totals[unit ^ turn, :, span] = lax.dot_general(
            weights[unit], attended[span], (((1,), (1,)), ((), ())), preferred_element_type=F32
        )
    for slot in range(2):
        out_ref[slot] = totals[slot].astype(BF16)


def project(route, own, beside, weight, pieces):
    tokens, width = own.shape
    rows = weight.shape[0]
    flat = [piece for pair in pieces for piece in pair]
    hbm = pl.BlockSpec(memory_space=pl.ANY)
    return pl.pallas_call(
        lambda *refs: project_kernel(
            *refs, rows=rows, pair_counts=[len(pair) for pair in pieces]
        ),
        in_specs=[pl.BlockSpec(memory_space=pltpu.SMEM)] + [hbm] * (3 + len(flat)),
        out_specs=pl.BlockSpec(memory_space=pltpu.VMEM),
        out_shape=jax.ShapeDtypeStruct((2, rows, 2 * tokens), BF16),
        scratch_shapes=[
            pltpu.VMEM((2 * tokens, width), BF16),
            pltpu.VMEM((2, rows, width), BF16),
            pltpu.VMEM((2, rows, 2 * tokens), F32),
            pltpu.SemaphoreType.DMA((3 + len(flat),)),
        ],
        compiler_params=pltpu.CompilerParams(vmem_limit_bytes=LESS_VMEM_BYTES),
        cost_estimate=pl.CostEstimate(
            flops=2_000_000_000, bytes_accessed=4 * 1024 * 1024, transcendentals=0
        ),
        name="project",
    )(route, own, beside, weight, *flat)


def finish_kernel(route_ref, *refs, starts, sizes):
    out_ref = refs[-1]
    kept = route_ref[2] == 1
    for index, (start, rows) in enumerate(zip(starts, sizes)):
        own, other = refs[2 * index : 2 * index + 2]

        @pl.when(kept)
        def _():
            out_ref[:, start : start + rows] = own[...].astype(F32).T.astype(BF16)

        @pl.when(jnp.logical_not(kept))
        def _():
            out_ref[:, start : start + rows] = other[...].astype(F32).T.astype(BF16)


def finish(route, sums, starts, sizes):
    vmem = pl.BlockSpec(memory_space=pltpu.VMEM)
    tokens = sums[0].shape[1]
    return pl.pallas_call(
        lambda *refs: finish_kernel(*refs, starts=starts, sizes=sizes),
        in_specs=[pl.BlockSpec(memory_space=pltpu.SMEM)] + [vmem] * len(sums),
        out_specs=vmem,
        out_shape=jax.ShapeDtypeStruct((tokens, sum(sizes)), BF16),
        compiler_params=pltpu.CompilerParams(vmem_limit_bytes=LESS_VMEM_BYTES),
        cost_estimate=SMALL_COST,
        name="finish",
    )(route, *sums)


def pick_kernel(self_ref, owner_ref, slot_ref, length_ref, pool_ref, *refs, capacity):
    outs, table = refs[:-1], refs[-1]
    requests = len(outs)
    own = self_ref[0]
    rows = pool_ref.shape[0]
    lane = lax.broadcasted_iota(jnp.int32, (8, rows), 1)
    row = lax.broadcasted_iota(jnp.int32, (8, rows), 0)
    for bit in range(requests):
        target = own ^ bit
        blocks = length_ref[target] // BT
        for rank in range(capacity):
            table[rank] = 0

        def note(block, count):
            owned = (owner_ref[target, block] == own) & (block < blocks)

            @pl.when(owned & (count < capacity))
            def _():
                table[count] = slot_ref[target, block]

            return count + owned.astype(jnp.int32)

        lax.fori_loop(0, BLK, note, jnp.int32(0), unroll=True)
        chosen = jnp.zeros((8, rows), F32)
        for rank in range(capacity):
            chosen = jnp.where((row == rank) & (lane == table[rank]), 1.0, chosen)
        outs[bit][...] = jnp.dot(
            chosen.astype(BF16), pool_ref[...], preferred_element_type=F32
        ).astype(BF16)


def pick(own_req, hit_owner, hit_slot, prefix_len, cache_pool, capacity):
    requests = hit_owner.shape[0]
    smem = pl.BlockSpec(memory_space=pltpu.SMEM)
    vmem = pl.BlockSpec(memory_space=pltpu.VMEM)
    return pl.pallas_call(
        lambda *refs: pick_kernel(*refs, capacity=capacity),
        in_specs=[smem] * 4 + [vmem],
        out_specs=[vmem] * requests,
        out_shape=[jax.ShapeDtypeStruct((8, cache_pool.shape[1]), BF16)] * requests,
        scratch_shapes=[pltpu.SMEM((capacity,), jnp.int32)],
        compiler_params=pltpu.CompilerParams(vmem_limit_bytes=VMEM_BYTES),
        cost_estimate=SMALL_COST,
        name="pick",
    )(own_req.reshape(1), hit_owner, hit_slot, prefix_len, cache_pool)


def after(value, *earlier):
    return lax.optimization_barrier((value, *earlier))[0] if earlier else value


def flip(size, bit):
    return [(index, index ^ bit) for index in range(size)]


def local(
    stretch_query,
    stretch_latent,
    cache_pool,
    hit_slot,
    hit_owner,
    prefix_len,
    head_mask,
    up_key,
    up_value,
    out_weight,
):
    groups = lax.axis_size("groups")
    req_count = lax.axis_size("req")
    head_count = lax.axis_size("head")
    capacity = max(2, (BLK + req_count - 1) // req_count * 3 // 2)
    own_req = lax.axis_index("req")
    own_head = lax.axis_index("head")
    paired = groups == 2 and req_count == 4 and head_count == 4 and sum(PIECES) == out_weight.shape[0]
    order = jnp.arange(req_count)
    partners = order ^ own_req if paired else order
    slots, picks, blocks = hit_tables(
        hit_slot, hit_owner, prefix_len, own_req, capacity, partners, 8 if paired else capacity
    )
    if not paired:
        outgoing = jnp.take(cache_pool, slots.reshape(-1), axis=0)
        incoming = lax.all_to_all(outgoing, "req", split_axis=0, concat_axis=0, tiled=True)
        prefix = jnp.dot(picks, incoming, preferred_element_type=F32).astype(BF16)
        gathered = lax.all_gather(prefix, "head", axis=0)
        pieces = [gathered[index] for index in range(head_count)]
        attended = attention(
            blocks, head_mask, stretch_query, stretch_latent, pieces, up_key, up_value
        )
        partial_out = lax.dot_general(
            attended,
            lax.all_gather(out_weight, "req", axis=0, tiled=True),
            (((1,), (1,)), ((), ())),
            preferred_element_type=F32,
        )
        return lax.psum_scatter(partial_out, "head", scatter_dimension=1, tiled=True).astype(BF16)

    own_group = lax.axis_index("groups")
    sizes = PIECES
    starts = [sum(sizes[:index]) for index in range(len(sizes))]

    def cut(chunk, *earlier):
        size = sizes[chunk]
        weights = after(out_weight, *earlier)
        if chunk >= WHOLE:
            return lax.slice_in_dim(weights, starts[chunk], starts[chunk] + size, axis=0)
        half = size // 2
        return lax.dynamic_slice_in_dim(weights, starts[chunk] + own_group * half, half, 0)

    def over_y(piece, *earlier):
        return lax.ppermute(after(piece, *earlier), "req", flip(req_count, 2))

    def over_x(piece, *earlier):
        return lax.ppermute(after(piece, *earlier), "groups", flip(groups, 1))

    def over_z(piece, bit):
        return lax.ppermute(piece, "head", flip(head_count, bit))

    outgoing = pick(own_req, hit_owner, hit_slot, prefix_len, cache_pool, capacity)
    incoming = [outgoing[0]] + [
        lax.ppermute(outgoing[bit], "req", flip(req_count, bit)) for bit in (1, 2, 3)
    ]
    y0 = over_y(cut(0, *outgoing))
    cuts = [cut(chunk, incoming[1]) for chunk in range(1, len(sizes))]
    owned = [
        cuts[chunk - 1]
        if chunk >= WHOLE
        else lax.slice_in_dim(
            after(out_weight, incoming[1]), starts[chunk], starts[chunk] + sizes[chunk], axis=0
        )
        for chunk in range(len(sizes))
    ]
    core = own_req & 1
    keeper = (own_head & 1) == core
    route = jnp.stack([(own_head >> 1) ^ (own_req >> 1), own_group, keeper]).astype(jnp.int32)
    prefix = jnp.dot(
        after(picks, route), jnp.concatenate(incoming, axis=0), preferred_element_type=F32
    ).astype(BF16)
    far = over_z(prefix, 2)
    near = over_z(prefix, 1)
    farther = over_z(after(far, near, *cuts, *owned), 1)
    x0 = over_x(y0, far)
    y1 = over_y(cuts[0], far)
    attended = attention(
        blocks,
        head_mask,
        stretch_query,
        stretch_latent,
        [prefix, near, far, farther],
        up_key,
        up_value,
    )
    beside = lax.ppermute(after(attended, x0, y1), "req", flip(req_count, 1))
    x1 = over_x(y1, attended)
    y2 = over_y(cuts[1], attended)
    y3 = over_y(cuts[2], attended)

    devices = [(req, head) for req in range(req_count) for head in range(head_count)]

    def place(req, head):
        return req * head_count + head

    to_keeper = [
        (place(req, head), place(req, head ^ 1)) for req, head in devices if (req ^ head) & 1
    ]
    to_far = [
        (place(req, head), place(req, head ^ 2)) for req, head in devices if not (req ^ head) & 1
    ]
    to_core = [
        (place(req, head), place(req ^ 1, head)) for req, head in devices if not (req ^ head) & 1
    ]
    axes = ("req", "head")

    bounds = [sum(STEPS[:index]) for index in range(len(STEPS) + 1)]
    spans = [
        (starts[first], sum(sizes[first:last])) for first, last in zip(bounds[:-1], bounds[1:])
    ]

    def send(chunk, pieces, *earlier):
        sums = project(after(route, *earlier), attended, beside, owned[chunk], pieces)
        return sums, lax.ppermute(sums, axes, to_keeper)

    def halve(sums, received):
        return (sums[1].astype(F32) + received[1].astype(F32)).astype(BF16)

    def pass_on(total):
        return lax.ppermute(total, axes, to_far)

    def settle(sums, received, passed):
        total = sums[0].astype(F32) + received[0].astype(F32) + passed.astype(F32)
        return total.astype(BF16)

    def split(total):
        own, other = total[:, :STRETCH], total[:, STRETCH:]
        return [own, lax.ppermute(other, axes, to_core)]

    sums0, got0 = send(0, [(y0, x0)])
    total0 = halve(sums0, got0)
    middle = sizes[0] // 2
    passed0 = [pass_on(total0[:middle]), pass_on(total0[middle:])]
    sums1, got1 = send(1, [(y1, x1)], sums0, y2)
    sums2, got2 = send(2, [(y2,)], sums1, total0)
    sums3, got3 = send(3, [(y3,)], sums2, passed0[0])
    total1 = halve(sums1, after(got1, sums3, passed0[1]))
    passed1 = pass_on(total1)
    total2 = halve(sums2, after(got2, total1))
    passed2 = pass_on(total2)
    total3 = halve(sums3, after(got3, total2))
    passed3 = pass_on(total3)
    passed0 = jnp.concatenate(passed0, axis=0)
    early = [
        settle(sums0, got0, after(passed0, total3)),
        settle(sums1, got1, after(passed1, total3)),
        settle(sums2, got2, after(passed2, total3)),
    ]
    settled = split(jnp.concatenate(early, axis=0)) + split(settle(sums3, got3, passed3))
    return finish(route, settled, (0, spans[3][0]), (spans[3][0], spans[3][1]))


def solution(mesh):
    placed = (
        P(("groups", "req"), "head"),
        P(("groups", "req"), None),
        P(("groups", "req"), "head"),
        P("groups", None),
        P("groups", None),
        P("groups"),
        P("head"),
        P(None, "head"),
        P(None, "head"),
        P("req", "head"),
    )
    return jax.shard_map(
        local, mesh=mesh, in_specs=placed, out_specs=P(("groups", "req"), "head"), check_vma=False
    )
```

```python
import math

import jax
import jax.numpy as jnp
from jax import lax
from jax.experimental import pallas as pl
from jax.experimental.pallas import tpu as pltpu
from jax.sharding import PartitionSpec as P

KVR = 512
NOPE = 128
VD = 128
BT = 64
STRETCH = 256
BLK = 16
LAT = 576
QKD = 192
ROPE = LAT - KVR
MASKED = -1e30
PIECES = (448, 416, 208, 208)
STEPS = (1, 1, 1, 1)
WHOLE = 2
VMEM_BYTES = 60 * 1024 * 1024
LESS_VMEM_BYTES = 20 * 1024 * 1024
SMALL_COST = pl.CostEstimate(flops=1024, bytes_accessed=1024, transcendentals=0)
BF16 = jnp.bfloat16
F32 = jnp.float32


def attention_kernel(blocks_ref, mask_ref, query_ref, stretch_ref, *refs, together, skipped):
    *pieces, key_ref, value_ref, out_ref, latent, rope = refs
    step = pl.program_id(0)
    prefix = sum(piece.shape[1] // LAT for piece in pieces) * BLK
    total = prefix + STRETCH

    @pl.when(step == 0)
    def _():
        lane = lax.broadcasted_iota(jnp.int32, (BLK, ROPE), 1)
        row = lax.broadcasted_iota(jnp.int32, (BLK, ROPE), 0)
        hidden = (lane == 0) & (row >= blocks_ref[0])
        extra = jnp.where(hidden, MASKED, 0.0).astype(BF16)
        places = [(piece, token) for piece in pieces for token in range(piece.shape[1] // LAT)]
        for index, (piece, token) in enumerate(places):
            start = index * BLK
            base = LAT * token
            latent[start : start + BLK, :] = piece[:, base : base + KVR]
            rope[start : start + BLK, :] = jnp.concatenate(
                [piece[:, base + KVR : base + LAT], extra], axis=1
            )
        latent[prefix:total, :] = stretch_ref[:, :KVR]
        rope[prefix:total, :] = jnp.concatenate(
            [stretch_ref[:, KVR:], jnp.zeros((STRETCH, ROPE), BF16)], axis=1
        )

    compressed = latent[...]
    keys = jnp.dot(compressed, key_ref[...], preferred_element_type=F32).astype(BF16)
    values = jnp.dot(compressed, value_ref[...], preferred_element_type=F32).astype(BF16)
    key_rope = rope[...]
    ones = jnp.ones((total, VD), BF16)
    lane = lax.broadcasted_iota(jnp.int32, (STRETCH, ROPE), 1)
    query_extra = jnp.where(lane == 0, 1.0, 0.0).astype(BF16)
    scale = 1.0 / (math.sqrt(QKD) * math.log(2.0))
    causal = lax.broadcasted_iota(jnp.int32, (STRETCH, STRETCH), 1) <= lax.broadcasted_iota(
        jnp.int32, (STRETCH, STRETCH), 0
    )
    for part in range(together):
        here = slice(part * VD, (part + 1) * VD)
        query = jnp.concatenate(
            [query_ref[:, part * QKD : (part + 1) * QKD], query_extra], axis=1
        )
        key = jnp.concatenate([keys[:, here], key_rope], axis=1)
        scores = lax.dot_general(
            query, key, (((1,), (1,)), ((), ())), preferred_element_type=F32
        )
        before = scores[:, :prefix]
        own = jnp.where(causal, scores[:, prefix:], MASKED)
        largest = jnp.maximum(
            jnp.max(before, axis=1, keepdims=True), jnp.max(own, axis=1, keepdims=True)
        )
        weights = jnp.concatenate(
            [
                jnp.exp2((before - largest) * scale).astype(BF16),
                jnp.exp2((own - largest) * scale).astype(BF16),
            ],
            axis=1,
        )
        value = jnp.concatenate([values[:, here], ones], axis=1)
        summed = jnp.dot(weights, value, preferred_element_type=F32)
        attended = (summed[:, :VD] / summed[:, VD:]).astype(BF16)
        kept = mask_ref[together * (step + skipped) + part].astype(F32).astype(BF16)
        out_ref[:, here] = attended * kept


def attention(blocks, head_mask, query, latent, pieces, up_key, up_value, part=0, parts=1):
    heads = up_key.shape[1] // NOPE // parts
    together = math.gcd(heads, 8)
    skipped = part * (heads // together)
    total = sum(piece.shape[1] // LAT for piece in pieces) * BLK + STRETCH

    def whole(array):
        return pl.BlockSpec(array.shape, lambda step: (0, 0))

    def columns(rows, width):
        return pl.BlockSpec((rows, together * width), lambda step: (0, step + skipped))

    smem = pl.BlockSpec(memory_space=pltpu.SMEM)
    return pl.pallas_call(
        lambda *refs: attention_kernel(*refs, together=together, skipped=skipped),
        grid=(heads // together,),
        in_specs=[smem, smem, columns(STRETCH, QKD)]
        + [whole(array) for array in [latent, *pieces]]
        + [columns(KVR, NOPE), columns(KVR, VD)],
        out_specs=pl.BlockSpec((STRETCH, together * VD), lambda step: (0, step)),
        out_shape=jax.ShapeDtypeStruct((STRETCH, heads * VD), BF16),
        scratch_shapes=[
            pltpu.VMEM((total, KVR), BF16),
            pltpu.VMEM((total, 2 * ROPE), BF16),
        ],
        compiler_params=pltpu.CompilerParams(vmem_limit_bytes=VMEM_BYTES),
        cost_estimate=pl.CostEstimate(
            flops=18_000_000_000 // parts, bytes_accessed=4 * 1024 * 1024, transcendentals=0
        ),
        name="attention",
    )(blocks, head_mask, query, latent, *pieces, up_key, up_value)


def hit_tables(hit_slot, hit_owner, prefix_len, own_req, capacity, sources, stride):
    block_index = jnp.arange(BLK)
    in_prefix = block_index[None, :] < (prefix_len // BT)[:, None]
    own_hits = in_prefix & (hit_owner == own_req)
    rank = jnp.cumsum(own_hits.astype(jnp.int32), axis=1) - 1
    chosen = own_hits[:, None, :] & (rank[:, None, :] == jnp.arange(capacity)[None, :, None])
    slots = jnp.sum(jnp.where(chosen, hit_slot[:, None, :], 0), axis=2)
    length = lax.dynamic_index_in_dim(prefix_len, own_req, 0, False)
    owners = lax.dynamic_index_in_dim(hit_owner, own_req, 0, False)
    from_source = (owners[:, None] == sources[None, :]) & (block_index < length // BT)[:, None]
    ranks = jnp.cumsum(from_source.astype(jnp.int32), axis=0) - 1
    picks = from_source[:, :, None] & (ranks[:, :, None] == jnp.arange(stride)[None, None, :])
    return slots, picks.reshape(BLK, -1).astype(BF16), (length // BT).reshape(1)


def refs_by_piece(refs, counts):
    refs = list(refs)
    return [[refs.pop(0) for _ in range(count)] for count in counts]


def project_kernel(route_ref, *refs, rows, pair_counts):
    own, beside, weight_hbm, refs = refs[0], refs[1], refs[2], refs[3:]
    pieces = refs[:-5]
    out_ref, attended, weights, totals, sems = refs[-5:]
    turn, group = route_ref[0], route_ref[1]
    tokens = own.shape[0]
    copies = [
        (own, attended.at[:tokens]),
        (weight_hbm, weights.at[0]),
        (beside, attended.at[tokens:]),
    ]
    place = 0
    for pair in refs_by_piece(pieces, pair_counts):
        size = sum(piece.shape[0] for piece in pair)
        for index, piece in enumerate(pair):
            half = piece.shape[0]
            offset = place + ((group if index == 0 else 1 - group) * half if len(pair) == 2 else 0)
            copies.append((piece, weights.at[1, pl.ds(pl.multiple_of(offset, 16), half)]))
        place += size
    copies = [
        pltpu.make_async_copy(source, target, sems.at[index])
        for index, (source, target) in enumerate(copies)
    ]
    last = tuple(range(3, len(copies)))
    needs = ((0, 0, (0, 1), (2,) + last), (0, 1, (2,), ()), (1, 0, last, ()), (1, 1, (), ()))
    for index in needs[0][2]:
        copies[index].start()
    for unit, request, awaited, following in needs:
        for index in awaited:
            copies[index].wait()
        for index in following:
            copies[index].start()
        span = slice(request * tokens, (request + 1) * tokens)
        totals[unit ^ turn, :, span] = lax.dot_general(
            weights[unit], attended[span], (((1,), (1,)), ((), ())), preferred_element_type=F32
        )
    for slot in range(2):
        out_ref[slot] = totals[slot].astype(BF16)


def project(route, own, beside, weight, pieces):
    tokens, width = own.shape
    rows = weight.shape[0]
    flat = [piece for pair in pieces for piece in pair]
    hbm = pl.BlockSpec(memory_space=pl.ANY)
    return pl.pallas_call(
        lambda *refs: project_kernel(
            *refs, rows=rows, pair_counts=[len(pair) for pair in pieces]
        ),
        in_specs=[pl.BlockSpec(memory_space=pltpu.SMEM)] + [hbm] * (3 + len(flat)),
        out_specs=pl.BlockSpec(memory_space=pltpu.VMEM),
        out_shape=jax.ShapeDtypeStruct((2, rows, 2 * tokens), BF16),
        scratch_shapes=[
            pltpu.VMEM((2 * tokens, width), BF16),
            pltpu.VMEM((2, rows, width), BF16),
            pltpu.VMEM((2, rows, 2 * tokens), F32),
            pltpu.SemaphoreType.DMA((3 + len(flat),)),
        ],
        compiler_params=pltpu.CompilerParams(vmem_limit_bytes=LESS_VMEM_BYTES),
        cost_estimate=pl.CostEstimate(
            flops=2_000_000_000, bytes_accessed=4 * 1024 * 1024, transcendentals=0
        ),
        name="project",
    )(route, own, beside, weight, *flat)


def finish_kernel(route_ref, *refs, starts, sizes):
    out_ref = refs[-1]
    kept = route_ref[2] == 1
    for index, (start, rows) in enumerate(zip(starts, sizes)):
        own, other = refs[2 * index : 2 * index + 2]

        @pl.when(kept)
        def _():
            out_ref[:, start : start + rows] = own[...].astype(F32).T.astype(BF16)

        @pl.when(jnp.logical_not(kept))
        def _():
            out_ref[:, start : start + rows] = other[...].astype(F32).T.astype(BF16)


def finish(route, sums, starts, sizes):
    vmem = pl.BlockSpec(memory_space=pltpu.VMEM)
    tokens = sums[0].shape[1]
    return pl.pallas_call(
        lambda *refs: finish_kernel(*refs, starts=starts, sizes=sizes),
        in_specs=[pl.BlockSpec(memory_space=pltpu.SMEM)] + [vmem] * len(sums),
        out_specs=vmem,
        out_shape=jax.ShapeDtypeStruct((tokens, sum(sizes)), BF16),
        compiler_params=pltpu.CompilerParams(vmem_limit_bytes=LESS_VMEM_BYTES),
        cost_estimate=SMALL_COST,
        name="finish",
    )(route, *sums)


def pick_kernel(self_ref, owner_ref, slot_ref, length_ref, pool_ref, *refs, capacity):
    outs, table = refs[:-1], refs[-1]
    requests = len(outs)
    own = self_ref[0]
    rows = pool_ref.shape[0]
    lane = lax.broadcasted_iota(jnp.int32, (8, rows), 1)
    row = lax.broadcasted_iota(jnp.int32, (8, rows), 0)
    for bit in range(requests):
        target = own ^ bit
        blocks = length_ref[target] // BT
        for rank in range(capacity):
            table[rank] = 0

        def note(block, count):
            owned = (owner_ref[target, block] == own) & (block < blocks)

            @pl.when(owned & (count < capacity))
            def _():
                table[count] = slot_ref[target, block]

            return count + owned.astype(jnp.int32)

        lax.fori_loop(0, BLK, note, jnp.int32(0), unroll=True)
        chosen = jnp.zeros((8, rows), F32)
        for rank in range(capacity):
            chosen = jnp.where((row == rank) & (lane == table[rank]), 1.0, chosen)
        outs[bit][...] = jnp.dot(
            chosen.astype(BF16), pool_ref[...], preferred_element_type=F32
        ).astype(BF16)


def pick(own_req, hit_owner, hit_slot, prefix_len, cache_pool, capacity):
    requests = hit_owner.shape[0]
    smem = pl.BlockSpec(memory_space=pltpu.SMEM)
    vmem = pl.BlockSpec(memory_space=pltpu.VMEM)
    return pl.pallas_call(
        lambda *refs: pick_kernel(*refs, capacity=capacity),
        in_specs=[smem] * 4 + [vmem],
        out_specs=[vmem] * requests,
        out_shape=[jax.ShapeDtypeStruct((8, cache_pool.shape[1]), BF16)] * requests,
        scratch_shapes=[pltpu.SMEM((capacity,), jnp.int32)],
        compiler_params=pltpu.CompilerParams(vmem_limit_bytes=VMEM_BYTES),
        cost_estimate=SMALL_COST,
        name="pick",
    )(own_req.reshape(1), hit_owner, hit_slot, prefix_len, cache_pool)


def after(value, *earlier):
    return lax.optimization_barrier((value, *earlier))[0] if earlier else value


def flip(size, bit):
    return [(index, index ^ bit) for index in range(size)]


def local(
    stretch_query,
    stretch_latent,
    cache_pool,
    hit_slot,
    hit_owner,
    prefix_len,
    head_mask,
    up_key,
    up_value,
    out_weight,
):
    groups = lax.axis_size("groups")
    req_count = lax.axis_size("req")
    head_count = lax.axis_size("head")
    capacity = max(2, (BLK + req_count - 1) // req_count * 3 // 2)
    own_req = lax.axis_index("req")
    own_head = lax.axis_index("head")
    paired = groups == 2 and req_count == 4 and head_count == 4 and sum(PIECES) == out_weight.shape[0]
    order = jnp.arange(req_count)
    partners = order ^ own_req if paired else order
    slots, picks, blocks = hit_tables(
        hit_slot, hit_owner, prefix_len, own_req, capacity, partners, 8 if paired else capacity
    )
    if not paired:
        outgoing = jnp.take(cache_pool, slots.reshape(-1), axis=0)
        incoming = lax.all_to_all(outgoing, "req", split_axis=0, concat_axis=0, tiled=True)
        prefix = jnp.dot(picks, incoming, preferred_element_type=F32).astype(BF16)
        gathered = lax.all_gather(prefix, "head", axis=0)
        pieces = [gathered[index] for index in range(head_count)]
        attended = attention(
            blocks, head_mask, stretch_query, stretch_latent, pieces, up_key, up_value
        )
        partial_out = lax.dot_general(
            attended,
            lax.all_gather(out_weight, "req", axis=0, tiled=True),
            (((1,), (1,)), ((), ())),
            preferred_element_type=F32,
        )
        return lax.psum_scatter(partial_out, "head", scatter_dimension=1, tiled=True).astype(BF16)

    own_group = lax.axis_index("groups")
    sizes = PIECES
    starts = [sum(sizes[:index]) for index in range(len(sizes))]

    def cut(chunk, *earlier):
        size = sizes[chunk]
        weights = after(out_weight, *earlier)
        if chunk >= WHOLE:
            return lax.slice_in_dim(weights, starts[chunk], starts[chunk] + size, axis=0)
        half = size // 2
        return lax.dynamic_slice_in_dim(weights, starts[chunk] + own_group * half, half, 0)

    def over_y(piece, *earlier):
        return lax.ppermute(after(piece, *earlier), "req", flip(req_count, 2))

    def over_x(piece, *earlier):
        return lax.ppermute(after(piece, *earlier), "groups", flip(groups, 1))

    def over_z(piece, bit):
        return lax.ppermute(piece, "head", flip(head_count, bit))

    outgoing = pick(own_req, hit_owner, hit_slot, prefix_len, cache_pool, capacity)
    incoming = [outgoing[0]] + [
        lax.ppermute(outgoing[bit], "req", flip(req_count, bit)) for bit in (1, 2, 3)
    ]
    y0 = over_y(cut(0, *outgoing))
    cuts = [cut(chunk, incoming[1]) for chunk in range(1, len(sizes))]
    owned = [
        cuts[chunk - 1]
        if chunk >= WHOLE
        else lax.slice_in_dim(
            after(out_weight, incoming[1]), starts[chunk], starts[chunk] + sizes[chunk], axis=0
        )
        for chunk in range(len(sizes))
    ]
    core = own_req & 1
    keeper = (own_head & 1) == core
    route = jnp.stack([(own_head >> 1) ^ (own_req >> 1), own_group, keeper]).astype(jnp.int32)
    picks = after(picks, route)
    gathered = jnp.concatenate(incoming, axis=0)
    width = gathered.shape[1] // 2
    prefix = [
        jnp.dot(picks, part, preferred_element_type=F32).astype(BF16)
        for part in (gathered[:, :width], gathered[:, width:])
    ]
    far = [over_z(part, 2) for part in prefix]
    near = [over_z(part, 1) for part in prefix]
    farther = [
        over_z(after(far[0], *cuts), 1),
        over_z(after(far[1], *near, *cuts, *owned), 1),
    ]
    x0 = over_x(y0, far[1])
    y1 = over_y(cuts[0], far[1])
    attended = attention(
        blocks,
        head_mask,
        stretch_query,
        stretch_latent,
        [*prefix, *near, *far, *farther],
        up_key,
        up_value,
    )
    beside = lax.ppermute(after(attended, x0, y1), "req", flip(req_count, 1))
    x1 = over_x(y1, attended)
    y2 = over_y(cuts[1], attended)
    y3 = over_y(cuts[2], attended)

    devices = [(req, head) for req in range(req_count) for head in range(head_count)]

    def place(req, head):
        return req * head_count + head

    to_keeper = [
        (place(req, head), place(req, head ^ 1)) for req, head in devices if (req ^ head) & 1
    ]
    to_far = [
        (place(req, head), place(req, head ^ 2)) for req, head in devices if not (req ^ head) & 1
    ]
    to_core = [
        (place(req, head), place(req ^ 1, head)) for req, head in devices if not (req ^ head) & 1
    ]
    axes = ("req", "head")

    bounds = [sum(STEPS[:index]) for index in range(len(STEPS) + 1)]
    spans = [
        (starts[first], sum(sizes[first:last])) for first, last in zip(bounds[:-1], bounds[1:])
    ]

    def send(chunk, pieces, *earlier):
        sums = project(after(route, *earlier), attended, beside, owned[chunk], pieces)
        return sums, lax.ppermute(sums, axes, to_keeper)

    def halve(sums, received):
        return (sums[1].astype(F32) + received[1].astype(F32)).astype(BF16)

    def pass_on(total):
        return lax.ppermute(total, axes, to_far)

    def settle(sums, received, passed):
        total = sums[0].astype(F32) + received[0].astype(F32) + passed.astype(F32)
        return total.astype(BF16)

    def split(total):
        own, other = total[:, :STRETCH], total[:, STRETCH:]
        return [own, lax.ppermute(other, axes, to_core)]

    sums0, got0 = send(0, [(y0, x0)])
    total0 = halve(sums0, got0)
    middle = sizes[0] // 2
    passed0 = [pass_on(total0[:middle]), pass_on(total0[middle:])]
    sums1, got1 = send(1, [(y1, x1)], sums0, y2)
    sums2, got2 = send(2, [(y2,)], sums1, total0)
    sums3, got3 = send(3, [(y3,)], sums2, passed0[0])
    total1 = halve(sums1, after(got1, sums3))
    passed1 = pass_on(total1)
    total2 = halve(sums2, after(got2, total1))
    passed2 = pass_on(total2)
    total3 = halve(sums3, after(got3, total2))
    passed3 = pass_on(total3)
    passed0 = jnp.concatenate(passed0, axis=0)
    early = [
        settle(sums0, got0, passed0),
        settle(sums1, got1, passed1),
        settle(sums2, got2, after(passed2, total3)),
    ]
    settled = split(jnp.concatenate(early, axis=0)) + split(settle(sums3, got3, passed3))
    return finish(route, settled, (0, spans[3][0]), (spans[3][0], spans[3][1]))


def solution(mesh):
    placed = (
        P(("groups", "req"), "head"),
        P(("groups", "req"), None),
        P(("groups", "req"), "head"),
        P("groups", None),
        P("groups", None),
        P("groups"),
        P("head"),
        P(None, "head"),
        P(None, "head"),
        P("req", "head"),
    )
    return jax.shard_map(
        local, mesh=mesh, in_specs=placed, out_specs=P(("groups", "req"), "head"), check_vma=False
    )
```

```python
import math

import jax
import jax.numpy as jnp
from jax import lax
from jax.experimental import pallas as pl
from jax.experimental.pallas import tpu as pltpu
from jax.sharding import PartitionSpec as P

KVR = 512
NOPE = 128
VD = 128
BT = 64
STRETCH = 256
BLK = 16
LAT = 576
QKD = 192
ROPE = LAT - KVR
MASKED = -1e30
PIECES = (448, 416, 208, 208)
STEPS = (1, 1, 1, 1)
WHOLE = 2
VMEM_BYTES = 60 * 1024 * 1024
LESS_VMEM_BYTES = 20 * 1024 * 1024
SMALL_COST = pl.CostEstimate(flops=1024, bytes_accessed=1024, transcendentals=0)
BF16 = jnp.bfloat16
F32 = jnp.float32


def attention_kernel(blocks_ref, mask_ref, query_ref, stretch_ref, *refs, together, skipped):
    *pieces, key_ref, value_ref, out_ref, latent, rope = refs
    step = pl.program_id(0)
    prefix = sum(piece.shape[1] // LAT for piece in pieces) * BLK
    total = prefix + STRETCH

    @pl.when(step == 0)
    def _():
        lane = lax.broadcasted_iota(jnp.int32, (BLK, ROPE), 1)
        row = lax.broadcasted_iota(jnp.int32, (BLK, ROPE), 0)
        hidden = (lane == 0) & (row >= blocks_ref[0])
        extra = jnp.where(hidden, MASKED, 0.0).astype(BF16)
        places = [(piece, token) for piece in pieces for token in range(piece.shape[1] // LAT)]
        for index, (piece, token) in enumerate(places):
            start = index * BLK
            base = LAT * token
            latent[start : start + BLK, :] = piece[:, base : base + KVR]
            rope[start : start + BLK, :] = jnp.concatenate(
                [piece[:, base + KVR : base + LAT], extra], axis=1
            )
        latent[prefix:total, :] = stretch_ref[:, :KVR]
        rope[prefix:total, :] = jnp.concatenate(
            [stretch_ref[:, KVR:], jnp.zeros((STRETCH, ROPE), BF16)], axis=1
        )

    compressed = latent[...]
    keys = jnp.dot(compressed, key_ref[...], preferred_element_type=F32).astype(BF16)
    values = jnp.dot(compressed, value_ref[...], preferred_element_type=F32).astype(BF16)
    key_rope = rope[...]
    ones = jnp.ones((total, VD), BF16)
    lane = lax.broadcasted_iota(jnp.int32, (STRETCH, ROPE), 1)
    query_extra = jnp.where(lane == 0, 1.0, 0.0).astype(BF16)
    scale = 1.0 / (math.sqrt(QKD) * math.log(2.0))
    causal = lax.broadcasted_iota(jnp.int32, (STRETCH, STRETCH), 1) <= lax.broadcasted_iota(
        jnp.int32, (STRETCH, STRETCH), 0
    )
    for part in range(together):
        here = slice(part * VD, (part + 1) * VD)
        query = jnp.concatenate(
            [query_ref[:, part * QKD : (part + 1) * QKD], query_extra], axis=1
        )
        key = jnp.concatenate([keys[:, here], key_rope], axis=1)
        scores = lax.dot_general(
            query, key, (((1,), (1,)), ((), ())), preferred_element_type=F32
        )
        before = scores[:, :prefix]
        own = jnp.where(causal, scores[:, prefix:], MASKED)
        largest = jnp.maximum(
            jnp.max(before, axis=1, keepdims=True), jnp.max(own, axis=1, keepdims=True)
        )
        weights = jnp.concatenate(
            [
                jnp.exp2((before - largest) * scale).astype(BF16),
                jnp.exp2((own - largest) * scale).astype(BF16),
            ],
            axis=1,
        )
        value = jnp.concatenate([values[:, here], ones], axis=1)
        summed = jnp.dot(weights, value, preferred_element_type=F32)
        attended = (summed[:, :VD] / summed[:, VD:]).astype(BF16)
        kept = mask_ref[together * (step + skipped) + part].astype(F32).astype(BF16)
        out_ref[:, here] = attended * kept


def attention(blocks, head_mask, query, latent, pieces, up_key, up_value, part=0, parts=1):
    heads = up_key.shape[1] // NOPE // parts
    together = math.gcd(heads, 8)
    skipped = part * (heads // together)
    total = sum(piece.shape[1] // LAT for piece in pieces) * BLK + STRETCH

    def whole(array):
        return pl.BlockSpec(array.shape, lambda step: (0, 0))

    def columns(rows, width):
        return pl.BlockSpec((rows, together * width), lambda step: (0, step + skipped))

    smem = pl.BlockSpec(memory_space=pltpu.SMEM)
    return pl.pallas_call(
        lambda *refs: attention_kernel(*refs, together=together, skipped=skipped),
        grid=(heads // together,),
        in_specs=[smem, smem, columns(STRETCH, QKD)]
        + [whole(array) for array in [latent, *pieces]]
        + [columns(KVR, NOPE), columns(KVR, VD)],
        out_specs=pl.BlockSpec((STRETCH, together * VD), lambda step: (0, step)),
        out_shape=jax.ShapeDtypeStruct((STRETCH, heads * VD), BF16),
        scratch_shapes=[
            pltpu.VMEM((total, KVR), BF16),
            pltpu.VMEM((total, 2 * ROPE), BF16),
        ],
        compiler_params=pltpu.CompilerParams(vmem_limit_bytes=VMEM_BYTES),
        cost_estimate=pl.CostEstimate(
            flops=18_000_000_000 // parts, bytes_accessed=4 * 1024 * 1024, transcendentals=0
        ),
        name="attention",
    )(blocks, head_mask, query, latent, *pieces, up_key, up_value)


def hit_tables(hit_slot, hit_owner, prefix_len, own_req, capacity, sources, stride):
    block_index = jnp.arange(BLK)
    in_prefix = block_index[None, :] < (prefix_len // BT)[:, None]
    own_hits = in_prefix & (hit_owner == own_req)
    rank = jnp.cumsum(own_hits.astype(jnp.int32), axis=1) - 1
    chosen = own_hits[:, None, :] & (rank[:, None, :] == jnp.arange(capacity)[None, :, None])
    slots = jnp.sum(jnp.where(chosen, hit_slot[:, None, :], 0), axis=2)
    length = lax.dynamic_index_in_dim(prefix_len, own_req, 0, False)
    owners = lax.dynamic_index_in_dim(hit_owner, own_req, 0, False)
    from_source = (owners[:, None] == sources[None, :]) & (block_index < length // BT)[:, None]
    ranks = jnp.cumsum(from_source.astype(jnp.int32), axis=0) - 1
    picks = from_source[:, :, None] & (ranks[:, :, None] == jnp.arange(stride)[None, None, :])
    return slots, picks.reshape(BLK, -1).astype(BF16), (length // BT).reshape(1)


def refs_by_piece(refs, counts):
    refs = list(refs)
    return [[refs.pop(0) for _ in range(count)] for count in counts]


def project_kernel(route_ref, *refs, rows, pair_counts):
    own, beside, weight_hbm, refs = refs[0], refs[1], refs[2], refs[3:]
    pieces = refs[:-5]
    out_ref, attended, weights, totals, sems = refs[-5:]
    turn, group = route_ref[0], route_ref[1]
    tokens = own.shape[0]
    copies = [
        (own, attended.at[:tokens]),
        (weight_hbm, weights.at[0]),
        (beside, attended.at[tokens:]),
    ]
    place = 0
    for pair in refs_by_piece(pieces, pair_counts):
        size = sum(piece.shape[0] for piece in pair)
        for index, piece in enumerate(pair):
            half = piece.shape[0]
            offset = place + ((group if index == 0 else 1 - group) * half if len(pair) == 2 else 0)
            copies.append((piece, weights.at[1, pl.ds(pl.multiple_of(offset, 16), half)]))
        place += size
    copies = [
        pltpu.make_async_copy(source, target, sems.at[index])
        for index, (source, target) in enumerate(copies)
    ]
    last = tuple(range(3, len(copies)))
    needs = ((0, 0, (0, 1), (2,) + last), (0, 1, (2,), ()), (1, 0, last, ()), (1, 1, (), ()))
    for index in needs[0][2]:
        copies[index].start()
    for unit, request, awaited, following in needs:
        for index in awaited:
            copies[index].wait()
        for index in following:
            copies[index].start()
        span = slice(request * tokens, (request + 1) * tokens)
        totals[unit ^ turn, :, span] = lax.dot_general(
            weights[unit], attended[span], (((1,), (1,)), ((), ())), preferred_element_type=F32
        )
    for slot in range(2):
        out_ref[slot] = totals[slot].astype(BF16)


def project(route, own, beside, weight, pieces):
    tokens, width = own.shape
    rows = weight.shape[0]
    flat = [piece for pair in pieces for piece in pair]
    hbm = pl.BlockSpec(memory_space=pl.ANY)
    return pl.pallas_call(
        lambda *refs: project_kernel(
            *refs, rows=rows, pair_counts=[len(pair) for pair in pieces]
        ),
        in_specs=[pl.BlockSpec(memory_space=pltpu.SMEM)] + [hbm] * (3 + len(flat)),
        out_specs=pl.BlockSpec(memory_space=pltpu.VMEM),
        out_shape=jax.ShapeDtypeStruct((2, rows, 2 * tokens), BF16),
        scratch_shapes=[
            pltpu.VMEM((2 * tokens, width), BF16),
            pltpu.VMEM((2, rows, width), BF16),
            pltpu.VMEM((2, rows, 2 * tokens), F32),
            pltpu.SemaphoreType.DMA((3 + len(flat),)),
        ],
        compiler_params=pltpu.CompilerParams(vmem_limit_bytes=LESS_VMEM_BYTES),
        cost_estimate=pl.CostEstimate(
            flops=2_000_000_000, bytes_accessed=4 * 1024 * 1024, transcendentals=0
        ),
        name="project",
    )(route, own, beside, weight, *flat)


def finish_kernel(route_ref, *refs, starts, sizes):
    out_ref = refs[-1]
    kept = route_ref[2] == 1
    for index, (start, rows) in enumerate(zip(starts, sizes)):
        own, other = refs[2 * index : 2 * index + 2]

        @pl.when(kept)
        def _():
            out_ref[:, start : start + rows] = own[...].astype(F32).T.astype(BF16)

        @pl.when(jnp.logical_not(kept))
        def _():
            out_ref[:, start : start + rows] = other[...].astype(F32).T.astype(BF16)


def finish(route, sums, starts, sizes):
    vmem = pl.BlockSpec(memory_space=pltpu.VMEM)
    tokens = sums[0].shape[1]
    return pl.pallas_call(
        lambda *refs: finish_kernel(*refs, starts=starts, sizes=sizes),
        in_specs=[pl.BlockSpec(memory_space=pltpu.SMEM)] + [vmem] * len(sums),
        out_specs=vmem,
        out_shape=jax.ShapeDtypeStruct((tokens, sum(sizes)), BF16),
        compiler_params=pltpu.CompilerParams(vmem_limit_bytes=LESS_VMEM_BYTES),
        cost_estimate=SMALL_COST,
        name="finish",
    )(route, *sums)


def pick_kernel(self_ref, owner_ref, slot_ref, length_ref, pool_ref, *refs, capacity):
    outs, table = refs[:-1], refs[-1]
    requests = len(outs)
    own = self_ref[0]
    rows = pool_ref.shape[0]
    lane = lax.broadcasted_iota(jnp.int32, (8, rows), 1)
    row = lax.broadcasted_iota(jnp.int32, (8, rows), 0)
    for bit in range(requests):
        target = own ^ bit
        blocks = length_ref[target] // BT
        for rank in range(capacity):
            table[rank] = 0

        def note(block, count):
            owned = (owner_ref[target, block] == own) & (block < blocks)

            @pl.when(owned & (count < capacity))
            def _():
                table[count] = slot_ref[target, block]

            return count + owned.astype(jnp.int32)

        lax.fori_loop(0, BLK, note, jnp.int32(0), unroll=True)
        chosen = jnp.zeros((8, rows), F32)
        for rank in range(capacity):
            chosen = jnp.where((row == rank) & (lane == table[rank]), 1.0, chosen)
        outs[bit][...] = jnp.dot(
            chosen.astype(BF16), pool_ref[...], preferred_element_type=F32
        ).astype(BF16)


def pick(own_req, hit_owner, hit_slot, prefix_len, cache_pool, capacity):
    requests = hit_owner.shape[0]
    smem = pl.BlockSpec(memory_space=pltpu.SMEM)
    vmem = pl.BlockSpec(memory_space=pltpu.VMEM)
    return pl.pallas_call(
        lambda *refs: pick_kernel(*refs, capacity=capacity),
        in_specs=[smem] * 4 + [vmem],
        out_specs=[vmem] * requests,
        out_shape=[jax.ShapeDtypeStruct((8, cache_pool.shape[1]), BF16)] * requests,
        scratch_shapes=[pltpu.SMEM((capacity,), jnp.int32)],
        compiler_params=pltpu.CompilerParams(vmem_limit_bytes=VMEM_BYTES),
        cost_estimate=SMALL_COST,
        name="pick",
    )(own_req.reshape(1), hit_owner, hit_slot, prefix_len, cache_pool)


def after(value, *earlier):
    return lax.optimization_barrier((value, *earlier))[0] if earlier else value


def flip(size, bit):
    return [(index, index ^ bit) for index in range(size)]


def local(
    stretch_query,
    stretch_latent,
    cache_pool,
    hit_slot,
    hit_owner,
    prefix_len,
    head_mask,
    up_key,
    up_value,
    out_weight,
):
    groups = lax.axis_size("groups")
    req_count = lax.axis_size("req")
    head_count = lax.axis_size("head")
    capacity = max(2, (BLK + req_count - 1) // req_count * 3 // 2)
    own_req = lax.axis_index("req")
    own_head = lax.axis_index("head")
    paired = groups == 2 and req_count == 4 and head_count == 4 and sum(PIECES) == out_weight.shape[0]
    order = jnp.arange(req_count)
    partners = order ^ own_req if paired else order
    slots, picks, blocks = hit_tables(
        hit_slot, hit_owner, prefix_len, own_req, capacity, partners, 8 if paired else capacity
    )
    if not paired:
        outgoing = jnp.take(cache_pool, slots.reshape(-1), axis=0)
        incoming = lax.all_to_all(outgoing, "req", split_axis=0, concat_axis=0, tiled=True)
        prefix = jnp.dot(picks, incoming, preferred_element_type=F32).astype(BF16)
        gathered = lax.all_gather(prefix, "head", axis=0)
        pieces = [gathered[index] for index in range(head_count)]
        attended = attention(
            blocks, head_mask, stretch_query, stretch_latent, pieces, up_key, up_value
        )
        partial_out = lax.dot_general(
            attended,
            lax.all_gather(out_weight, "req", axis=0, tiled=True),
            (((1,), (1,)), ((), ())),
            preferred_element_type=F32,
        )
        return lax.psum_scatter(partial_out, "head", scatter_dimension=1, tiled=True).astype(BF16)

    own_group = lax.axis_index("groups")
    sizes = PIECES
    starts = [sum(sizes[:index]) for index in range(len(sizes))]

    def cut(chunk, *earlier):
        size = sizes[chunk]
        weights = after(out_weight, *earlier)
        if chunk >= WHOLE:
            return lax.slice_in_dim(weights, starts[chunk], starts[chunk] + size, axis=0)
        half = size // 2
        return lax.dynamic_slice_in_dim(weights, starts[chunk] + own_group * half, half, 0)

    def over_y(piece, *earlier):
        return lax.ppermute(after(piece, *earlier), "req", flip(req_count, 2))

    def over_x(piece, *earlier):
        return lax.ppermute(after(piece, *earlier), "groups", flip(groups, 1))

    def over_z(piece, bit):
        return lax.ppermute(piece, "head", flip(head_count, bit))

    outgoing = pick(own_req, hit_owner, hit_slot, prefix_len, cache_pool, capacity)
    incoming = [outgoing[0]] + [
        lax.ppermute(outgoing[bit], "req", flip(req_count, bit)) for bit in (1, 2, 3)
    ]
    y0 = over_y(cut(0, *outgoing))
    cuts = [cut(chunk, incoming[1]) for chunk in range(1, len(sizes))]
    owned = [
        cuts[chunk - 1]
        if chunk >= WHOLE
        else lax.slice_in_dim(
            after(out_weight, incoming[1]), starts[chunk], starts[chunk] + sizes[chunk], axis=0
        )
        for chunk in range(len(sizes))
    ]
    core = own_req & 1
    keeper = (own_head & 1) == core
    route = jnp.stack([(own_head >> 1) ^ (own_req >> 1), own_group, keeper]).astype(jnp.int32)
    picks = after(picks, route)
    gathered = jnp.concatenate(incoming, axis=0)
    width = gathered.shape[1] // 2
    prefix = [
        jnp.dot(picks, part, preferred_element_type=F32).astype(BF16)
        for part in (gathered[:, :width], gathered[:, width:])
    ]
    far = [over_z(part, 2) for part in prefix]
    near = [over_z(part, 1) for part in prefix]
    farther = [
        over_z(far[0], 1),
        over_z(after(far[1], *near, *cuts, *owned), 1),
    ]
    x0 = over_x(y0, far[1])
    y1 = over_y(cuts[0], far[1])
    attended = attention(
        blocks,
        head_mask,
        stretch_query,
        stretch_latent,
        [*prefix, *near, *far, *farther],
        up_key,
        up_value,
    )
    beside = lax.ppermute(after(attended, x0, y1), "req", flip(req_count, 1))
    x1 = over_x(y1, attended)
    y2 = over_y(cuts[1], attended)
    y3 = over_y(cuts[2], attended)

    devices = [(req, head) for req in range(req_count) for head in range(head_count)]

    def place(req, head):
        return req * head_count + head

    to_keeper = [
        (place(req, head), place(req, head ^ 1)) for req, head in devices if (req ^ head) & 1
    ]
    to_far = [
        (place(req, head), place(req, head ^ 2)) for req, head in devices if not (req ^ head) & 1
    ]
    to_core = [
        (place(req, head), place(req ^ 1, head)) for req, head in devices if not (req ^ head) & 1
    ]
    axes = ("req", "head")

    bounds = [sum(STEPS[:index]) for index in range(len(STEPS) + 1)]
    spans = [
        (starts[first], sum(sizes[first:last])) for first, last in zip(bounds[:-1], bounds[1:])
    ]

    def send(chunk, pieces, *earlier):
        sums = project(after(route, *earlier), attended, beside, owned[chunk], pieces)
        return sums, lax.ppermute(sums, axes, to_keeper)

    def halve(sums, received):
        return (sums[1].astype(F32) + received[1].astype(F32)).astype(BF16)

    def pass_on(total):
        return lax.ppermute(total, axes, to_far)

    def settle(sums, received, passed):
        total = sums[0].astype(F32) + received[0].astype(F32) + passed.astype(F32)
        return total.astype(BF16)

    def split(total):
        own, other = total[:, :STRETCH], total[:, STRETCH:]
        return [own, lax.ppermute(other, axes, to_core)]

    sums0, got0 = send(0, [(y0, x0)])
    total0 = halve(sums0, got0)
    middle = sizes[0] // 2
    passed0 = [pass_on(total0[:middle]), pass_on(total0[middle:])]
    sums1, got1 = send(1, [(y1, x1)], sums0, y2)
    sums2, got2 = send(2, [(y2,)], sums1, total0)
    sums3, got3 = send(3, [(y3,)], sums2, passed0[0])
    total1 = halve(sums1, after(got1, sums3))
    passed1 = pass_on(total1)
    total2 = halve(sums2, after(got2, total1))
    passed2 = pass_on(total2)
    total3 = halve(sums3, after(got3, total2))
    passed3 = pass_on(total3)
    passed0 = jnp.concatenate(passed0, axis=0)
    early = [
        settle(sums0, got0, passed0),
        settle(sums1, got1, passed1),
        settle(sums2, got2, after(passed2, total3)),
    ]
    settled = split(jnp.concatenate(early, axis=0)) + split(settle(sums3, got3, passed3))
    return finish(route, settled, (0, spans[3][0]), (spans[3][0], spans[3][1]))


def solution(mesh):
    placed = (
        P(("groups", "req"), "head"),
        P(("groups", "req"), None),
        P(("groups", "req"), "head"),
        P("groups", None),
        P("groups", None),
        P("groups"),
        P("head"),
        P(None, "head"),
        P(None, "head"),
        P("req", "head"),
    )
    return jax.shard_map(
        local, mesh=mesh, in_specs=placed, out_specs=P(("groups", "req"), "head"), check_vma=False
    )
```
